128 devices in a mesh: group: 4 (over y_hi, core), member: 32 (over z, y_lo, x).
Axes of the slice: x: 4, y: 4 (y_hi: 2, y_lo: 2; y = y_hi * 2 + y_lo), z: 4, core: 2. Of those that a mesh axis runs over, the one named last changes fastest.
Arguments:
- activations: bfloat16 [4096, 7, 7, 2048], P(('group', 'member')), may hold values from -24 to 24
- shuffle: int32 [4096], replicated, may hold values from 0 to 4095, as said below
- pointer: int32 [1], replicated, may hold values from 0 to 65535
- conv_reduce: bfloat16 [2048, 512], replicated, may hold values from -0.125 to 0.125
- conv_spatial: bfloat16 [3, 3, 512, 512], replicated, may hold values from -0.09375 to 0.09375
- conv_expand: bfloat16 [512, 2048], replicated, may hold values from -0.25 to 0.25
- key_head: bfloat16 [2048, 128], replicated, may hold values from -0.125 to 0.125
- queries: bfloat16 [4096, 128], P(('group', 'member')), may hold values from -6 to 6
- negative_memory: bfloat16 [65536, 128], P('member'), may hold values from -0.5 to 0.5
Outputs:
- logits: bfloat16 [4096, 65536], P('group', 'member')
- matching_pair_similarity: float32 [4096], P(('group', 'member'))
- new_queue: bfloat16 [65536, 128], P('member')
The draws below stay inside these ranges and needn't reach their ends.
Inputs may be any that keep to these rules, and one draw needn't show every extreme that they name: `shuffle`: a permutation of 0 to 4095 that maps each aligned block of 1024 rows onto itself; the 32 rows of each device come from every device of that block, 1 row from each.
All inputs are finite; a program needn't handle non-finite values.
Results may differ from the reference program's by a relative error of at most 0.01.
Values may be sent and summed in bfloat16 or wider, within the bound.
No kernel may reach another device: no remote copies, remote signals or barrier semaphores. Data moves between devices by JAX's collectives and lax.ppermute only.
A program may use at most 128 MiB of HBM per device.

```python
import math
import jax
import jax.numpy as jnp
from jax import lax

D_OUT = 2048
D_MID = 512
KEY = 128
IMG_DEV = 32
BATCH = 4096
QUEUE = 65536
N_GROUP = 4
N_MEMBER = 32


def draw_activations(key, part):
    key = jax.random.fold_in(key, 3)
    key_list = jax.random.split(key, 3)
    shape = (BATCH, 7, 7, D_OUT)
    scale = jnp.exp(jax.random.uniform(key_list[0], (BATCH, 1, 1, 1), jnp.float32, math.log(0.25), math.log(3.0)))
    base = jnp.clip(jax.random.normal(key_list[1], shape, jnp.float32), -4.0, 4.0)
    channel = jnp.exp(jax.random.uniform(key_list[2], (BATCH, 1, 1, D_OUT), jnp.float32, math.log(0.5), math.log(2.0)))
    return (base * scale * channel).astype(jnp.bfloat16)


def draw_shuffle(key, part):
    key = jax.random.fold_in(key, 7)
    per_peer = IMG_DEV // N_MEMBER

    def one_group(group_key, group_id):
        key_list = jax.random.split(group_key, 4)
        member_ids = jnp.arange(N_MEMBER, dtype=jnp.int32)
        slot_ids = jnp.arange(IMG_DEV, dtype=jnp.int32)
        relabel = jax.random.permutation(key_list[0], N_MEMBER)
        offsets = jax.random.permutation(key_list[1], N_MEMBER)
        source_member = relabel[jnp.mod(offsets[:, None] + slot_ids[None, :], N_MEMBER)]
        row_lookup_tables = jax.vmap(lambda one_key: jax.random.permutation(one_key, IMG_DEV))(jax.random.split(key_list[2], N_MEMBER))
        source_row = row_lookup_tables[source_member, member_ids[:, None] * per_peer + slot_ids[None, :] // N_MEMBER]
        mixing = jax.vmap(lambda one_key: jax.random.permutation(one_key, IMG_DEV))(jax.random.split(key_list[3], N_MEMBER))
        global_rows = jnp.take_along_axis(source_member * IMG_DEV + source_row, mixing, axis=1)
        return (global_rows + group_id * N_MEMBER * IMG_DEV).reshape(-1)
    drawn = jax.vmap(one_group)(jax.random.split(key, N_GROUP), jnp.arange(N_GROUP, dtype=jnp.int32))
    return drawn.reshape(-1).astype(jnp.int32)


def block_levels(stream_key, dims, shards, low, high):
    gain = 1.0
    for axis_at, blocks in shards:
        heights = jax.random.uniform(jax.random.fold_in(jax.random.fold_in(stream_key, 6), axis_at), (blocks,), jnp.float32, low / len(shards), high / len(shards))
        gain = gain * jnp.repeat(jnp.exp(heights), dims[axis_at] // blocks).reshape((-1,) + (1,) * (len(dims) - 1 - axis_at))
    return gain


def bell_draw(stream_key, shape, deviation, bound, pieces=(), kind=jnp.bfloat16):
    values = jax.random.normal(stream_key, shape, jnp.float32) * deviation
    if len(pieces) > 0:
        values = block_levels(stream_key, shape, pieces, -0.22, 0.18) * values
    return jnp.clip(values, min=-bound, max=bound).astype(kind)


def setup_inputs(seed: int = 0) -> dict:
    seeds = jax.random.split(jax.random.key(seed), 10)
    activations = draw_activations(jax.random.fold_in(seeds[9], 71), 0)
    shuffle = draw_shuffle(jax.random.fold_in(seeds[9], 71), 0)
    pointer = jax.random.randint(seeds[2], (1,), 0, QUEUE).astype(jnp.int32)
    conv_reduce = bell_draw(seeds[3], (D_OUT, D_MID), D_OUT ** -0.5, 0.125)
    conv_spatial = bell_draw(seeds[4], (3, 3, D_MID, D_MID), (9 * D_MID) ** -0.5, 0.09375)
    conv_expand = bell_draw(seeds[5], (D_MID, D_OUT), D_MID ** -0.5, 0.25)
    key_head = bell_draw(seeds[6], (D_OUT, KEY), D_OUT ** -0.5, 0.125)
    queries = bell_draw(seeds[7], (BATCH, KEY), 1.0, 6.0, ((0, 128),))
    negative_memory = bell_draw(seeds[8], (QUEUE, KEY), KEY ** -0.5, 0.5, ((0, 32),))
    return {"activations": activations, "shuffle": shuffle, "pointer": pointer, "conv_reduce": conv_reduce, "conv_spatial": conv_spatial, "conv_expand": conv_expand, "key_head": key_head, "queries": queries, "negative_memory": negative_memory}


norm_eps = 1e-05
unit_eps = 1e-06
sharpness_divisor = 0.2

def standardize(values):
    center = lax.optimization_barrier(jnp.mean(values, axis=0))
    spread = lax.optimization_barrier(jnp.mean(values * values, axis=0)) - center * center
    return (values - center) * lax.rsqrt(spread + norm_eps)

def encode(rows, conv_reduce, conv_spatial, conv_expand, key_head):
    row_count = rows.shape[0]
    flat = rows.reshape(row_count * 49, rows.shape[3])
    first = jnp.dot(flat, conv_reduce, preferred_element_type=jnp.float32)
    reduced = jnp.maximum(standardize(first), 0.0).astype(jnp.bfloat16)
    reduced = reduced.reshape(row_count, 7, 7, reduced.shape[1])
    padded = jnp.pad(reduced, ((0, 0), (1, 1), (1, 1), (0, 0)))
    second = jnp.zeros((row_count * 49, conv_spatial.shape[3]), jnp.float32)
    for shift_y in range(3):
        for shift_x in range(3):
            window = padded[:, shift_y:shift_y + 7, shift_x:shift_x + 7, :].reshape(row_count * 49, -1)
            second = second + jnp.dot(window, conv_spatial[shift_y, shift_x], preferred_element_type=jnp.float32)
    spatial = jnp.maximum(standardize(second), 0.0).astype(jnp.bfloat16)
    third = jnp.dot(spatial, conv_expand, preferred_element_type=jnp.float32)
    merged = jnp.maximum(standardize(third) + flat.astype(jnp.float32), 0.0)
    pooled = lax.optimization_barrier(jnp.mean(merged.reshape(row_count, 49, -1), axis=1)).astype(jnp.bfloat16)
    projected = jnp.dot(pooled, key_head, preferred_element_type=jnp.float32)
    return (projected * lax.rsqrt(lax.optimization_barrier(jnp.sum(projected * projected, axis=1, keepdims=True)) + unit_eps)).astype(jnp.bfloat16)

def reference(activations, shuffle, pointer, conv_reduce, conv_spatial, conv_expand, key_head, queries, negative_memory):
    blocks = shuffle.reshape(BATCH // IMG_DEV, IMG_DEV)

    def one_block(indices):
        return encode(activations[indices], conv_reduce, conv_spatial, conv_expand, key_head)
    mixed_keys = lax.map(one_block, blocks).reshape(BATCH, KEY)
    embedded_targets = jnp.zeros((BATCH, KEY), jnp.bfloat16).at[shuffle].set(mixed_keys)
    query_f = queries.astype(jnp.float32)
    narrow_waist_layer = (query_f * lax.rsqrt(lax.optimization_barrier(jnp.sum(query_f * query_f, axis=1, keepdims=True)) + unit_eps)).astype(jnp.bfloat16)

    def score_block(skip_connection_layer):
        similarity_matrix = jnp.dot(skip_connection_layer, negative_memory.T, preferred_element_type=jnp.float32) / sharpness_divisor
        return similarity_matrix.astype(jnp.bfloat16)
    logits = lax.map(score_block, narrow_waist_layer.reshape(BATCH // IMG_DEV, IMG_DEV, KEY)).reshape(BATCH, QUEUE)
    matching_pair_similarity = lax.optimization_barrier(jnp.sum(narrow_waist_layer.astype(jnp.float32) * embedded_targets.astype(jnp.float32), axis=1)) / sharpness_divisor
    slot_ids = jnp.mod(pointer[0] + jnp.arange(BATCH, dtype=jnp.int32), QUEUE).astype(jnp.int32)
    new_queue = negative_memory.at[slot_ids].set(embedded_targets)
    return (logits, matching_pair_similarity, new_queue)
```

```python
import jax
import jax.numpy as jnp
from jax import lax
from jax.experimental import pallas as pl
from jax.experimental.pallas import tpu as pltpu
from jax.sharding import PartitionSpec as P

norm_eps = 1e-05
unit_eps = 1e-06
sharpness_divisor = 0.2

IMAGES = 32
SIDE = 7
POSITIONS = SIDE * SIDE
ROW = SIDE * IMAGES
ROWS = POSITIONS * IMAGES
MID = 512
OUT = 2048
KEY = 128
SLAB = 16
MIB = 1 << 20
f32 = jnp.float32
bf16 = jnp.bfloat16


def iota(shape, dim):
    return lax.broadcasted_iota(jnp.int32, shape, dim)


def dot(a, b):
    return jnp.dot(a, b, preferred_element_type=f32)


def dot_tn(a, b):
    return lax.dot_general(a, b, (((0,), (0,)), ((), ())), preferred_element_type=f32)


def dot_nt(a, b):
    return lax.dot_general(a, b, (((1,), (1,)), ((), ())), preferred_element_type=f32)


def spread_select(select):
    size = IMAGES * SLAB
    left = (iota((size, IMAGES), 0) // SLAB == iota((size, IMAGES), 1)).astype(bf16)
    right = (iota((IMAGES, size), 0) == iota((IMAGES, size), 1) % IMAGES).astype(bf16)
    spread = dot(dot(left, select).astype(bf16), right)
    same = iota((size, size), 0) % SLAB == iota((size, size), 1) // IMAGES
    return jnp.where(same, spread, 0.0).astype(bf16)


def split(value):
    high = value.astype(bf16)
    return high, (value - high.astype(f32)).astype(bf16)


def unit_of(queries):
    query_f = queries.astype(f32)
    return query_f * lax.rsqrt(jnp.sum(query_f * query_f, axis=1, keepdims=True) + unit_eps)


def reduce_kernel(
    place_ref, x_ref, weight_ref, table_ref, query_ref,
    delta_ref, mean_ref, select_ref, message_ref, first, total,
):
    step = pl.program_id(0)
    part = dot(x_ref[...], weight_ref[...])
    first[pl.ds(pl.multiple_of(step * ROW, ROW), ROW), :] = part
    image_sum = jnp.sum(part.reshape(SIDE, IMAGES, MID), axis=0)

    @pl.when(step == 0)
    def _():
        total[...] = image_sum

    @pl.when(step > 0)
    def _():
        total[...] += image_sum

    @pl.when(step == SIDE - 1)
    def _():
        mean = (total[...] * (1.0 / POSITIONS)).astype(bf16)
        mean_f = mean.astype(f32)
        mean_ref[...] = mean
        for y in range(SIDE):
            rows = pl.ds(y * ROW, ROW)
            centered = first[rows, :].reshape(SIDE, IMAGES, MID) - mean_f[None]
            delta_ref[rows, :] = centered.reshape(ROW, MID).astype(bf16)
        table = table_ref[pl.ds(pl.multiple_of(place_ref[0] * IMAGES, IMAGES), IMAGES), :]
        local = table - (place_ref[0] * (IMAGES * IMAGES) + place_ref[1] * IMAGES)
        mine = jnp.logical_and(local >= 0, local < IMAGES)
        chosen = jnp.sum(jnp.where(mine, local, 0), axis=1, keepdims=True)
        select = (chosen == iota((IMAGES, IMAGES), 1)).astype(bf16)
        select_ref[...] = select
        mover = spread_select(select)
        size = SLAB * IMAGES
        for slab in range(3):
            moved = dot(mover, delta_ref[pl.ds(slab * size, size), :])
            message_ref[:, pl.ds(slab * SLAB, SLAB), :] = moved.reshape(IMAGES, SLAB, MID).astype(bf16)
        last = jnp.concatenate([delta_ref[pl.ds(3 * size, IMAGES), :], mean], axis=0)
        moved = dot(mover[:, : 2 * IMAGES], last).reshape(IMAGES, SLAB, MID)
        unit = unit_of(query_ref[...])
        unit = jnp.concatenate([unit[8 * k : 8 * k + 8] for k in range(4)], axis=1)
        moved = jnp.concatenate(
            [moved[:, :8, :], jnp.broadcast_to(unit[None], (IMAGES, 8, MID))], axis=1
        )
        message_ref[:, pl.ds(3 * SLAB, SLAB), :] = moved.astype(bf16)


def store_windows(windows, reduced, y):
    edge = jnp.zeros((IMAGES, MID), bf16)
    at = (y + 1) * ROW
    windows[pl.ds(at, IMAGES), pl.ds(0, MID)] = edge
    windows[pl.ds(at + IMAGES, ROW - IMAGES), pl.ds(0, MID)] = reduced[: ROW - IMAGES]
    windows[pl.ds(at, ROW), pl.ds(MID, MID)] = reduced
    windows[pl.ds(at, ROW - IMAGES), pl.ds(2 * MID, MID)] = reduced[IMAGES:]
    windows[pl.ds(at + ROW - IMAGES, IMAGES), pl.ds(2 * MID, MID)] = edge


def clear_border(windows):
    border = jnp.zeros((ROW, 3 * MID), bf16)
    windows[pl.ds(0, ROW), :] = border
    windows[pl.ds((SIDE + 1) * ROW, ROW), :] = border


def convolve_row(windows, spatial_weight, y):
    return (
        dot(windows[pl.ds(y * ROW, ROW), :], spatial_weight[0])
        + dot(windows[pl.ds((y + 1) * ROW, ROW), :], spatial_weight[1])
        + dot(windows[pl.ds((y + 2) * ROW, ROW), :], spatial_weight[2])
    )


def fold(value):
    return jnp.sum(value.reshape(-1, IMAGES, value.shape[1]), axis=0)


def centered_spread(values, center):
    total = jnp.zeros((IMAGES, values.shape[1]), f32)
    for y in range(SIDE):
        away = values[pl.ds(y * ROW, ROW), :] - center
        total = total + fold(away * away)
    return jnp.sum(total, axis=0, keepdims=True) * (1.0 / ROWS)


def block_kernel(
    received_ref, spatial_hbm, expand_hbm, message_ref, units_ref,
    values, windows, spatial, spatial_weight, expand_weight, sems,
):
    load_spatial = pltpu.make_async_copy(spatial_hbm, spatial_weight, sems.at[0])
    load_expand = pltpu.make_async_copy(expand_hbm, expand_weight, sems.at[1])
    load_spatial.start()
    load_expand.start()

    size = SLAB * IMAGES
    row, column = iota((size, size), 0), iota((size, size), 1)
    mover = jnp.logical_and(row % IMAGES == column // SLAB, row // IMAGES == column % SLAB).astype(bf16)
    tail = received_ref[:, pl.ds(3 * SLAB, SLAB), :]
    last = dot(mover[: 2 * IMAGES], tail.reshape(size, MID))
    mean = last[IMAGES:]
    total = jnp.zeros((IMAGES, MID), f32)
    for slab in range(3):
        moved = dot(mover, received_ref[:, pl.ds(slab * SLAB, SLAB), :].reshape(size, MID))
        moved = (moved.reshape(SLAB, IMAGES, MID) + mean[None]).reshape(size, MID)
        values[pl.ds(slab * size, size), :] = moved
        total = total + fold(moved)
    values[pl.ds(3 * size, IMAGES), :] = last[:IMAGES] + mean
    total = total + last[:IMAGES] + mean

    units = tail.astype(f32)[:, 8:, :]
    units = jnp.concatenate(
        [units[:, None, :, k * KEY : (k + 1) * KEY] for k in range(4)], axis=1
    )
    units_ref[...] = units.reshape(IMAGES * IMAGES, KEY).astype(bf16)

    center1 = jnp.sum(total, axis=0, keepdims=True) * (1.0 / ROWS)
    scale1 = lax.rsqrt(centered_spread(values, center1) + norm_eps)
    clear_border(windows)
    for y in range(SIDE):
        reduced = jnp.maximum((values[pl.ds(y * ROW, ROW), :] - center1) * scale1, 0.0)
        store_windows(windows, reduced.astype(bf16), y)

    load_spatial.wait()
    total = jnp.zeros((IMAGES, MID), f32)
    for y in range(SIDE):
        second = convolve_row(windows, spatial_weight, y)
        values[pl.ds(y * ROW, ROW), :] = second
        total = total + fold(second)
    center2 = jnp.sum(total, axis=0, keepdims=True) * (1.0 / ROWS)
    scale2 = lax.rsqrt(centered_spread(values, center2) + norm_eps)
    total = jnp.zeros((IMAGES, MID), f32)
    for y in range(SIDE):
        rows = pl.ds(y * ROW, ROW)
        kept = jnp.maximum((values[rows, :] - center2) * scale2, 0.0).astype(bf16)
        spatial[rows, :] = kept
        total = total + fold(kept.astype(f32))
    spatial_mean = jnp.sum(total, axis=0, keepdims=True) * (1.0 / ROWS)

    load_expand.wait()
    scale3 = []
    for part in range(OUT // MID):
        columns = pl.ds(part * MID, MID)
        total = jnp.zeros((IMAGES, MID), f32)
        for y in range(SIDE):
            third = dot(spatial[pl.ds(y * ROW, ROW), :], expand_weight[:, columns])
            values[pl.ds(y * ROW, ROW), :] = third
            total = total + fold(third)
        center3 = jnp.sum(total, axis=0, keepdims=True) * (1.0 / ROWS)
        scale3.append(lax.rsqrt(centered_spread(values, center3) + norm_eps))

    parts = []
    for value in (center1, scale1, center2, scale2, spatial_mean):
        parts += [piece.astype(f32) for piece in split(value)]
    parts += scale3
    parts.append(jnp.zeros((SLAB - len(parts), MID), f32))
    message = jnp.concatenate(parts, axis=0)
    message_ref[...] = jnp.broadcast_to(message[None], (IMAGES, SLAB, MID)).astype(bf16)


def home_kernel(
    received_ref, select_ref, delta_ref, mean_ref, query_ref, head_ref, x_hbm, spatial_hbm, expand_hbm,
    key_ref, similarity_ref,
    windows, x, spatial, spatial_weight, expand_weight, pooled, sems,
):
    load_spatial = pltpu.make_async_copy(spatial_hbm, spatial_weight, sems.at[0])
    load_expand = pltpu.make_async_copy(expand_hbm, expand_weight, sems.at[1])
    load_x = pltpu.make_async_copy(x_hbm, x, sems.at[2])
    load_spatial.start()
    load_expand.start()
    load_x.start()

    size = SLAB * IMAGES
    mover = spread_select(select_ref[...])
    stats = dot_tn(mover, received_ref[...].reshape(size, MID)).reshape(SLAB, IMAGES, MID)
    offset1 = mean_ref[...].astype(f32) - (stats[0] + stats[1])
    scale1 = stats[2] + stats[3]
    center2 = stats[4] + stats[5]
    scale2 = stats[6] + stats[7]
    mean_high, mean_low = stats[8].astype(bf16), stats[9].astype(bf16)

    clear_border(windows)
    for y in range(SIDE):
        delta = delta_ref[pl.ds(y * ROW, ROW), :].astype(f32).reshape(SIDE, IMAGES, MID)
        reduced = jnp.maximum((delta + offset1[None]) * scale1[None], 0.0)
        store_windows(windows, reduced.reshape(ROW, MID).astype(bf16), y)

    load_spatial.wait()
    for y in range(SIDE):
        second = convolve_row(windows, spatial_weight, y).reshape(SIDE, IMAGES, MID)
        kept = jnp.maximum((second - center2[None]) * scale2[None], 0.0)
        spatial[pl.ds(y * ROW, ROW), :] = kept.reshape(ROW, MID).astype(bf16)

    load_expand.wait()
    load_x.wait()
    for part in range(OUT // MID):
        columns = pl.ds(part * MID, MID)
        weight = expand_weight[:, columns]
        center3 = dot(mean_high, weight) + dot(mean_low, weight)
        scale3 = stats[10 + part]
        total = jnp.zeros((IMAGES, MID), f32)
        for y in range(SIDE):
            rows = pl.ds(y * ROW, ROW)
            third = dot(spatial[rows, :], weight).reshape(SIDE, IMAGES, MID)
            kept = x[rows, columns].astype(f32).reshape(SIDE, IMAGES, MID)
            merged = jnp.maximum((third - center3[None]) * scale3[None] + kept, 0.0)
            total = total + jnp.sum(merged, axis=0)
        pooled[:, columns] = (total * (1.0 / POSITIONS)).astype(bf16)
    projected = dot(pooled[...], head_ref[...])
    key = projected * lax.rsqrt(jnp.sum(projected * projected, axis=1, keepdims=True) + unit_eps)
    key = key.astype(bf16)
    unit = unit_of(query_ref[...]).astype(bf16)
    pairs = dot_nt(unit, key)
    own = iota((IMAGES, IMAGES), 0) == iota((IMAGES, IMAGES), 1)
    similarity_ref[...] = jnp.sum(jnp.where(own, pairs, 0.0), axis=0, keepdims=True) / sharpness_divisor
    key_ref[...] = jnp.broadcast_to(key[None], key_ref.shape)


def queue_kernel(place_ref, near_ref, far_ref, memory_ref, out_ref, padded):
    slots = memory_ref.shape[0]
    batch = IMAGES * 128
    core = place_ref[2]
    start = place_ref[3]
    edge = jnp.zeros((slots, KEY), bf16)
    padded[pl.ds(0, slots), :] = edge
    padded[pl.ds(slots + batch, slots), :] = edge
    padded[pl.ds(2 * slots + batch, SLAB), :] = edge[:SLAB]
    half = IMAGES * IMAGES
    for high in range(2):
        for ref, which in ((near_ref, core), (far_ref, 1 - core)):
            at = pl.multiple_of(slots + (2 * high + which) * half, half)
            padded[pl.ds(at, half), :] = ref[pl.ds(high * IMAGES, IMAGES)].reshape(half, KEY)
    tile = 256
    base = start // SLAB * SLAB
    inner = start - base
    pick = (iota((tile, tile + SLAB), 1) == iota((tile, tile + SLAB), 0) + inner).astype(bf16)
    for part in range(slots // tile):
        rows = padded[pl.ds(pl.multiple_of(base + part * tile, SLAB), tile + SLAB), :]
        fresh = dot(pick, rows)
        index = start - slots + part * tile + iota((tile, KEY), 0)
        inside = jnp.logical_and(index >= 0, index < batch)
        old = memory_ref[pl.ds(part * tile, tile), :].astype(f32)
        out_ref[pl.ds(part * tile, tile), :] = jnp.where(inside, fresh, old).astype(bf16)


def params(mib):
    return pltpu.CompilerParams(vmem_limit_bytes=mib * MIB)


VMEM = pl.BlockSpec(memory_space=pltpu.VMEM)
SMEM = pl.BlockSpec(memory_space=pltpu.SMEM)
HBM = pl.BlockSpec(memory_space=pl.ANY)


def shape(*dims, dtype=bf16):
    return jax.ShapeDtypeStruct(dims, dtype)


def reduce_call(place, x, conv_reduce, table, queries):
    whole = lambda dims: pl.BlockSpec(dims, lambda step: (0,) * len(dims))
    return pl.pallas_call(
        reduce_kernel,
        grid=(SIDE,),
        in_specs=[
            SMEM,
            pl.BlockSpec((ROW, OUT), lambda step: (step, 0)),
            whole((OUT, MID)),
            whole(table.shape),
            whole((IMAGES, KEY)),
        ],
        out_specs=[
            whole((ROWS, MID)),
            whole((IMAGES, MID)),
            whole((IMAGES, IMAGES)),
            whole((IMAGES, 4 * SLAB, MID)),
        ],
        out_shape=[
            shape(ROWS, MID),
            shape(IMAGES, MID),
            shape(IMAGES, IMAGES),
            shape(IMAGES, 4 * SLAB, MID),
        ],
        scratch_shapes=[pltpu.VMEM((ROWS, MID), f32), pltpu.VMEM((IMAGES, MID), f32)],
        compiler_params=params(40),
        name="reduce",
    )(place, x, conv_reduce, table, queries)


def block_call(received, conv_spatial, conv_expand):
    return pl.pallas_call(
        block_kernel,
        in_specs=[VMEM, HBM, HBM],
        out_specs=[VMEM, VMEM],
        out_shape=[shape(IMAGES, SLAB, MID), shape(IMAGES * IMAGES, KEY)],
        scratch_shapes=[
            pltpu.VMEM((ROWS, MID), f32),
            pltpu.VMEM((ROWS + 2 * ROW, 3 * MID), bf16),
            pltpu.VMEM((ROWS, MID), bf16),
            pltpu.VMEM((3, 3 * MID, MID), bf16),
            pltpu.VMEM((MID, OUT), bf16),
            pltpu.SemaphoreType.DMA((2,)),
        ],
        compiler_params=params(48),
        name="block",
    )(received, conv_spatial, conv_expand)


def home_call(received, select, delta, mean, queries, key_head, x, conv_spatial, conv_expand, copies):
    return pl.pallas_call(
        home_kernel,
        in_specs=[VMEM] * 6 + [HBM] * 3,
        out_specs=[VMEM, VMEM],
        out_shape=[shape(copies, IMAGES, KEY), shape(1, IMAGES, dtype=f32)],
        scratch_shapes=[
            pltpu.VMEM((ROWS + 2 * ROW, 3 * MID), bf16),
            pltpu.VMEM((ROWS, OUT), bf16),
            pltpu.VMEM((ROWS, MID), bf16),
            pltpu.VMEM((3, 3 * MID, MID), bf16),
            pltpu.VMEM((MID, OUT), bf16),
            pltpu.VMEM((IMAGES, OUT), bf16),
            pltpu.SemaphoreType.DMA((3,)),
        ],
        compiler_params=params(48),
        name="home",
    )(received, select, delta, mean, queries, key_head, x, conv_spatial, conv_expand)


def queue_call(place, near, far, memory):
    return pl.pallas_call(
        queue_kernel,
        in_specs=[SMEM] + [VMEM] * 3,
        out_specs=VMEM,
        out_shape=shape(*memory.shape),
        scratch_shapes=[pltpu.VMEM((2 * memory.shape[0] + IMAGES * 128 + SLAB, KEY), bf16)],
        compiler_params=params(32),
        name="queue",
    )(place, near, far, memory)


def per_device(
    activations, shuffle, pointer, conv_reduce, conv_spatial, conv_expand, key_head, queries, negative_memory
):
    group, member = lax.axis_index("group"), lax.axis_index("member")
    members = lax.axis_size("member")
    slots = negative_memory.shape[0]
    total_slots = slots * members
    batch = shuffle.shape[0]
    offset = jnp.mod(member * slots - pointer[0], total_slots)
    wrapped = jnp.where(offset > total_slots - slots, offset - total_slots, batch)
    start = slots + jnp.where(offset < batch, offset, wrapped)
    place = jnp.stack([group, member, group % 2, start]).astype(jnp.int32)

    x = activations.transpose(1, 2, 0, 3).reshape(ROWS, OUT)
    spatial_weight = conv_spatial.reshape(3, 3 * MID, MID)
    table = shuffle.reshape(batch // IMAGES, IMAGES)
    delta, mean, select, message = reduce_call(place, x, conv_reduce, table, queries)
    received = lax.all_to_all(message, "member", split_axis=0, concat_axis=0, tiled=True)
    moments, units = block_call(received, spatial_weight, conv_expand)
    returned = lax.all_to_all(moments, "member", split_axis=0, concat_axis=0, tiled=True)
    logits = (dot_nt(units, negative_memory) / sharpness_divisor).astype(bf16)
    copies, similarity = home_call(
        returned, select, delta, mean, queries, key_head, x, spatial_weight, conv_expand, 2 * members
    )
    same_core = [[g * members + m for g in (core, core + 2) for m in range(members)] for core in (0, 1)]
    near = lax.all_to_all(
        copies, ("group", "member"), split_axis=0, concat_axis=0, tiled=True, axis_index_groups=same_core
    )
    far = lax.ppermute(near, "group", [(0, 1), (1, 0), (2, 3), (3, 2)])
    new_queue = queue_call(place, near, far, negative_memory)
    return logits, similarity.reshape(IMAGES), new_queue


def solution(mesh):
    placed = (
        P(("group", "member"), None, None, None),
        P(),
        P(),
        P(),
        P(),
        P(),
        P(),
        P(("group", "member"), None),
        P("member", None),
    )
    return jax.shard_map(
        per_device,
        mesh=mesh,
        in_specs=placed,
        out_specs=(P("group", "member"), P(("group", "member")), P("member", None)),
        check_vma=False,
    )
```

```python
import jax
import jax.numpy as jnp
from jax import lax
from jax.experimental import pallas as pl
from jax.experimental.pallas import tpu as pltpu
from jax.sharding import PartitionSpec as P

norm_eps = 1e-05
unit_eps = 1e-06
sharpness_divisor = 0.2

IMAGES = 32
SIDE = 7
POSITIONS = SIDE * SIDE
ROW = SIDE * IMAGES
ROWS = POSITIONS * IMAGES
MID = 512
OUT = 2048
KEY = 128
SLAB = 8
SLABS = POSITIONS // SLAB
SIZE = SLAB * IMAGES
LAST = SLABS * MID
QUERIES = LAST + KEY
MESSAGE = QUERIES + MID
MOMENTS = 6 * KEY
MIB = 1 << 20
f32 = jnp.float32
bf16 = jnp.bfloat16


def iota(shape, dim):
    return lax.broadcasted_iota(jnp.int32, shape, dim)


def dot(a, b):
    return jnp.dot(a, b, preferred_element_type=f32)


def dot_tn(a, b):
    return lax.dot_general(a, b, (((0,), (0,)), ((), ())), preferred_element_type=f32)


def dot_nt(a, b):
    return lax.dot_general(a, b, (((1,), (1,)), ((), ())), preferred_element_type=f32)


def spread_select(select):
    left = (iota((SIZE, IMAGES), 0) // SLAB == iota((SIZE, IMAGES), 1)).astype(bf16)
    right = (iota((IMAGES, SIZE), 0) == iota((IMAGES, SIZE), 1) % IMAGES).astype(bf16)
    spread = dot(dot(left, select).astype(bf16), right)
    same = iota((SIZE, SIZE), 0) % SLAB == iota((SIZE, SIZE), 1) // IMAGES
    return jnp.where(same, spread, 0.0).astype(bf16)


def quarters(value):
    return jnp.concatenate([value[:, k * KEY : (k + 1) * KEY] for k in range(4)], axis=0)


def whole(pieces):
    return jnp.concatenate([pieces[k] for k in range(4)], axis=1)


def split(value):
    high = value.astype(bf16).astype(f32)
    return high, value - high


def unit_of(queries):
    query_f = queries.astype(f32)
    return query_f * lax.rsqrt(jnp.sum(query_f * query_f, axis=1, keepdims=True) + unit_eps)


def start_all(pairs, sems):
    copies = [pltpu.make_async_copy(a, b, sems.at[k]) for k, (a, b) in enumerate(pairs)]
    for copy in copies:
        copy.start()
    return copies


def peer_selector(place_ref, table):
    per_row = KEY // IMAGES
    block_rows = table[pl.ds(pl.multiple_of(place_ref[0] * SLAB, SLAB), SLAB), :]
    local = block_rows - (place_ref[0] * (IMAGES * IMAGES) + place_ref[1] * IMAGES)
    mine = jnp.logical_and(local >= 0, local < IMAGES)
    found = jnp.where(mine, local, 0).astype(f32).astype(bf16)
    by_block = (iota((IMAGES, SLAB), 0) // per_row == iota((IMAGES, SLAB), 1)).astype(bf16)
    inside = iota((IMAGES, KEY), 1) // IMAGES == iota((IMAGES, KEY), 0) % per_row
    chosen = jnp.sum(jnp.where(inside, dot(by_block, found), 0.0), axis=1, keepdims=True)
    return (chosen == iota((IMAGES, IMAGES), 1).astype(f32)).astype(bf16)


def reduce_kernel(
    place_ref, x_hbm, weight_hbm, table_hbm, query_hbm, spatial_hbm, expand_hbm,
    x, spatial_weight, expand_weight, delta, mean_ref, select_ref, message,
    weight, table, query, sems,
):
    map_rows = [pl.ds(y * ROW, ROW) for y in range(SIDE)]
    weight_rows = [pl.ds(k * MID, MID) for k in range(OUT // MID)]
    loads = start_all(
        [(table_hbm, table), (query_hbm, query)]
        + [(weight_hbm.at[rows, :], weight.at[rows, :]) for rows in weight_rows]
        + [(x_hbm.at[rows, :], x.at[rows, :]) for rows in map_rows]
        + [(spatial_hbm.at[k], spatial_weight.at[k]) for k in range(3)]
        + [(expand_hbm, expand_weight)],
        sems,
    )

    loads[0].wait()
    loads[1].wait()
    select = peer_selector(place_ref, table)
    select_ref[...] = select
    mover = spread_select(select)
    unit = unit_of(query[...])
    unit = jnp.concatenate([unit[SLAB * k : SLAB * (k + 1)] for k in range(4)], axis=1)
    message[:, :, pl.ds(QUERIES, MID)] = jnp.broadcast_to(unit[None], (IMAGES, SLAB, MID)).astype(bf16)
    for copy in loads[2:6]:
        copy.wait()
    done = [0]
    parts = []

    def finish(y):
        delta[map_rows[y], :] = (parts[y] - mean_f[None]).reshape(ROW, MID).astype(bf16)
        while (done[0] + 1) * SLAB <= (y + 1) * SIDE:
            moved = dot(mover, delta[pl.ds(done[0] * SIZE, SIZE), :]).reshape(IMAGES, SLAB, MID)
            message[:, :, pl.ds(done[0] * MID, MID)] = moved.astype(bf16)
            done[0] += 1

    for y in range(SIDE):
        for k in {0: [0], 1: [1, 2, 3], 4: [4, 5, 6]}.get(y, ()):
            loads[6 + k].wait()
        part = dot(x[map_rows[y], :], weight[...]).reshape(SIDE, IMAGES, MID)
        if y == 0:
            mean = (jnp.sum(part, axis=0) * (1.0 / SIDE)).astype(bf16)
            mean_f = mean.astype(f32)
            mean_ref[...] = mean
        if y > 0:
            finish(y - 1)
        parts.append(part)
    finish(SIDE - 1)
    last = jnp.concatenate([quarters(delta[pl.ds(SLABS * SIZE, IMAGES), :]), quarters(mean)], axis=0)
    message[:, :, pl.ds(LAST, KEY)] = dot(mover, last).reshape(IMAGES, SLAB, KEY).astype(bf16)
    for copy in loads[6 + SIDE :]:
        copy.wait()


def store_windows(windows, reduced, y):
    edge = jnp.zeros((IMAGES, MID), bf16)
    at = (y + 1) * ROW
    windows[pl.ds(at, IMAGES), pl.ds(0, MID)] = edge
    windows[pl.ds(at + IMAGES, ROW - IMAGES), pl.ds(0, MID)] = reduced[: ROW - IMAGES]
    windows[pl.ds(at, ROW), pl.ds(MID, MID)] = reduced
    windows[pl.ds(at, ROW - IMAGES), pl.ds(2 * MID, MID)] = reduced[IMAGES:]
    windows[pl.ds(at + ROW - IMAGES, IMAGES), pl.ds(2 * MID, MID)] = edge


def clear_border(windows):
    border = jnp.zeros((ROW, 3 * MID), bf16)
    windows[pl.ds(0, ROW), :] = border
    windows[pl.ds((SIDE + 1) * ROW, ROW), :] = border


def convolve_row(windows, spatial_weight, y):
    return (
        dot(windows[pl.ds(y * ROW, ROW), :], spatial_weight[0])
        + dot(windows[pl.ds((y + 1) * ROW, ROW), :], spatial_weight[1])
        + dot(windows[pl.ds((y + 2) * ROW, ROW), :], spatial_weight[2])
    )


def fold(value):
    return jnp.sum(value.reshape(-1, IMAGES, value.shape[1]), axis=0)


def block_mean(total):
    return jnp.sum(total, axis=0, keepdims=True) * (1.0 / ROWS)


def block_kernel(received, spatial_weight, expand_weight, moments, units, values, windows, spatial):
    clear_border(windows)
    row, column = iota((SIZE, SIZE), 0), iota((SIZE, SIZE), 1)
    mover = jnp.logical_and(row % IMAGES == column // SLAB, row // IMAGES == column % SLAB).astype(bf16)

    tail = dot(mover, received[:, :, pl.ds(LAST, KEY)].reshape(SIZE, KEY)).reshape(SLAB, IMAGES, KEY)
    mean = whole(tail[4:])
    shift = jnp.sum(mean, axis=0, keepdims=True) * (1.0 / IMAGES)
    away = mean - shift
    last = whole(tail[:4]) + away
    values[pl.ds(SLABS * SIZE, IMAGES), :] = last
    total, squares = last, last * last
    for slab in range(SLABS):
        moved = dot(mover, received[:, :, pl.ds(slab * MID, MID)].reshape(SIZE, MID))
        moved = (moved.reshape(SLAB, IMAGES, MID) + away[None]).reshape(SIZE, MID)
        values[pl.ds(slab * SIZE, SIZE), :] = moved
        total = total + fold(moved)
        squares = squares + fold(moved * moved)
    offset1 = block_mean(total)
    center1 = shift + offset1
    scale1 = lax.rsqrt(block_mean(squares) - offset1 * offset1 + norm_eps).astype(bf16).astype(f32)
    for y in range(SIDE):
        reduced = jnp.maximum((values[pl.ds(y * ROW, ROW), :] - offset1) * scale1, 0.0)
        store_windows(windows, reduced.astype(bf16), y)

    queries = received[:, :, pl.ds(QUERIES, MID)].astype(f32)
    queries = jnp.concatenate([queries[:, None, :, k * KEY : (k + 1) * KEY] for k in range(4)], axis=1)
    units[...] = queries.reshape(IMAGES * IMAGES, KEY).astype(bf16)

    total = squares = jnp.zeros((IMAGES, MID), f32)
    for y in range(SIDE):
        second = convolve_row(windows, spatial_weight, y)
        values[pl.ds(y * ROW, ROW), :] = second
        total = total + fold(second)
        squares = squares + fold(second * second)
    center2 = block_mean(total)
    scale2 = lax.rsqrt(block_mean(squares) - center2 * center2 + norm_eps).astype(bf16).astype(f32)
    total = jnp.zeros((IMAGES, MID), f32)
    for y in range(SIDE):
        rows = pl.ds(y * ROW, ROW)
        kept = jnp.maximum((values[rows, :] - center2) * scale2, 0.0).astype(bf16)
        spatial[rows, :] = kept
        total = total + fold(kept.astype(f32))
    mean_high, mean_low = split(block_mean(total))

    scale3 = []
    for part in range(OUT // MID):
        weight = expand_weight[:, pl.ds(part * MID, MID)]
        center3 = dot(mean_high.astype(bf16), weight) + dot(mean_low.astype(bf16), weight)
        squares = jnp.zeros((IMAGES, MID), f32)
        for y in range(SIDE):
            third = dot(spatial[pl.ds(y * ROW, ROW), :], weight)
            squares = squares + fold(third * third)
        scale3.append(lax.rsqrt(block_mean(squares) - center3 * center3 + norm_eps))

    vectors = [*split(center1), *split(center2), mean_high, mean_low, scale1, scale2, *scale3]
    vectors = [quarters(vector) for vector in vectors]
    tiles = [jnp.concatenate(vectors[k : k + 2], axis=0) for k in range(0, 12, 2)]
    packed = jnp.concatenate(tiles, axis=1)
    moments[...] = jnp.broadcast_to(packed[None], (IMAGES, SLAB, MOMENTS)).astype(bf16)


def home_kernel(
    received, select, mean, delta, spatial_weight, expand_weight, x, head, query,
    keys, similarity_ref, windows, spatial, pooled,
):
    clear_border(windows)
    stats = dot_tn(spread_select(select[...]), received[...].reshape(SIZE, MOMENTS))
    stats = stats.reshape(SLAB, IMAGES, MOMENTS)
    vectors = []
    for k in range(12):
        half, lanes = 4 * (k % 2), k // 2 * KEY
        vectors.append(whole([stats[half + q, :, lanes : lanes + KEY] for q in range(4)]))
    offset1 = mean[...].astype(f32) - (vectors[0] + vectors[1])
    center2 = vectors[2] + vectors[3]
    mean_high, mean_low = vectors[4].astype(bf16), vectors[5].astype(bf16)
    scale1, scale2 = vectors[6], vectors[7]

    for y in range(SIDE):
        away = delta[pl.ds(y * ROW, ROW), :].astype(f32).reshape(SIDE, IMAGES, MID)
        reduced = jnp.maximum((away + offset1[None]) * scale1[None], 0.0)
        store_windows(windows, reduced.reshape(ROW, MID).astype(bf16), y)

    for y in range(SIDE):
        second = convolve_row(windows, spatial_weight, y).reshape(SIDE, IMAGES, MID)
        kept = jnp.maximum((second - center2[None]) * scale2[None], 0.0)
        spatial[pl.ds(y * ROW, ROW), :] = kept.reshape(ROW, MID).astype(bf16)

    for part in range(OUT // MID):
        columns = pl.ds(part * MID, MID)
        weight = expand_weight[:, columns]
        center3 = dot(mean_high, weight) + dot(mean_low, weight)
        scale3 = vectors[8 + part]
        total = jnp.zeros((IMAGES, MID), f32)
        for y in range(SIDE):
            rows = pl.ds(y * ROW, ROW)
            third = dot(spatial[rows, :], weight).reshape(SIDE, IMAGES, MID)
            kept = x[rows, columns].astype(f32).reshape(SIDE, IMAGES, MID)
            merged = jnp.maximum((third - center3[None]) * scale3[None] + kept, 0.0)
            total = total + jnp.sum(merged, axis=0)
        pooled[:, columns] = (total * (1.0 / POSITIONS)).astype(bf16)
    projected = dot(pooled[...], head[...])
    key = projected * lax.rsqrt(jnp.sum(projected * projected, axis=1, keepdims=True) + unit_eps)
    key = key.astype(bf16)
    keys[...] = jnp.broadcast_to(key[None], keys.shape)
    unit = unit_of(query[...]).astype(bf16)
    pairs = dot_nt(unit, key)
    own = iota((IMAGES, IMAGES), 0) == iota((IMAGES, IMAGES), 1)
    similarity_ref[...] = jnp.sum(jnp.where(own, pairs, 0.0), axis=0, keepdims=True) / sharpness_divisor


def logits_kernel(units_ref, memory_ref, out_ref):
    out_ref[...] = (dot_nt(units_ref[...], memory_ref[...]) * (1.0 / sharpness_divisor)).astype(bf16)


def queue_kernel(place_ref, near_hbm, far_hbm, memory_hbm, out_ref, padded, memory, sems):
    slots = memory.shape[0]
    batch = 4 * IMAGES * IMAGES
    half = IMAGES * IMAGES
    core = place_ref[2]
    start = place_ref[3]
    pairs = [(memory_hbm, memory)]
    for high in range(2):
        for ref, which in ((near_hbm, core), (far_hbm, 1 - core)):
            at = pl.multiple_of(slots + (2 * high + which) * half, half)
            pairs.append((ref.at[pl.ds(high * half, half), :], padded.at[pl.ds(at, half), :]))
    loads = start_all(pairs, sems)
    edge = jnp.zeros((slots, KEY), bf16)
    padded[pl.ds(0, slots), :] = edge
    padded[pl.ds(slots + batch, slots), :] = edge
    padded[pl.ds(2 * slots + batch, ALIGN), :] = edge[:ALIGN]
    base = start // ALIGN * ALIGN
    inner = start - base
    pick = (iota((TILE, TILE + ALIGN), 1) == iota((TILE, TILE + ALIGN), 0) + inner).astype(bf16)
    for copy in loads:
        copy.wait()
    for part in range(slots // TILE):
        rows = padded[pl.ds(pl.multiple_of(base + part * TILE, ALIGN), TILE + ALIGN), :]
        fresh = dot(pick, rows)
        index = start - slots + part * TILE + iota((TILE, KEY), 0)
        inside = jnp.logical_and(index >= 0, index < batch)
        old = memory[pl.ds(part * TILE, TILE), :].astype(f32)
        out_ref[pl.ds(part * TILE, TILE), :] = jnp.where(inside, fresh, old).astype(bf16)


ALIGN = 16
TILE = 256


def params(mib):
    return pltpu.CompilerParams(vmem_limit_bytes=mib * MIB)


VMEM = pl.BlockSpec(memory_space=pltpu.VMEM)
SMEM = pl.BlockSpec(memory_space=pltpu.SMEM)
ANY = pl.BlockSpec(memory_space=pl.ANY)
HBM = pl.BlockSpec(memory_space=pltpu.HBM)


def shape(*dims, dtype=bf16):
    return jax.ShapeDtypeStruct(dims, dtype)


def scratch(*dims, dtype=bf16):
    return pltpu.VMEM(dims, dtype)


def dma(count):
    return pltpu.SemaphoreType.DMA((count,))


def in_hbm(*arrays):
    return [pltpu.with_memory_space_constraint(array, pltpu.HBM) for array in arrays]


def in_vmem(*arrays):
    return [pltpu.with_memory_space_constraint(array, pltpu.VMEM) for array in arrays]


def reduce_call(place, x, conv_reduce, table, queries, conv_spatial, conv_expand):
    return pl.pallas_call(
        reduce_kernel,
        in_specs=[SMEM] + [HBM] * 6,
        out_specs=[VMEM] * 7,
        out_shape=[
            scratch(ROWS, OUT),
            scratch(*conv_spatial.shape),
            scratch(MID, OUT),
            scratch(ROWS, MID),
            scratch(IMAGES, MID),
            scratch(IMAGES, IMAGES),
            scratch(IMAGES, SLAB, MESSAGE),
        ],
        scratch_shapes=[
            scratch(OUT, MID),
            scratch(*table.shape, dtype=jnp.int32),
            scratch(IMAGES, KEY),
            dma(10 + SIDE),
        ],
        compiler_params=params(24),
        name="reduce",
    )(place, *in_hbm(x, conv_reduce, table, queries, conv_spatial, conv_expand))


def block_call(received, spatial_weight, expand_weight):
    return pl.pallas_call(
        block_kernel,
        in_specs=[VMEM] * 3,
        out_specs=[VMEM, VMEM],
        out_shape=[scratch(IMAGES, SLAB, MOMENTS), scratch(IMAGES * IMAGES, KEY)],
        scratch_shapes=[
            scratch(ROWS, MID, dtype=f32),
            scratch(ROWS + 2 * ROW, 3 * MID),
            scratch(ROWS, MID),
        ],
        compiler_params=params(30),
        name="block",
    )(*in_vmem(received, spatial_weight, expand_weight))


def home_call(received, select, mean, delta, spatial_weight, expand_weight, x, key_head, queries, copies):
    return pl.pallas_call(
        home_kernel,
        in_specs=[VMEM] * 9,
        out_specs=[VMEM, VMEM],
        out_shape=[scratch(copies, IMAGES, KEY), shape(1, IMAGES, dtype=f32)],
        scratch_shapes=[
            scratch(ROWS + 2 * ROW, 3 * MID),
            scratch(ROWS, MID),
            scratch(IMAGES, OUT),
        ],
        compiler_params=params(30),
        name="home",
    )(*in_vmem(received, select, mean, delta, spatial_weight, expand_weight, x), key_head, queries)


def logits_call(units, memory):
    rows, columns = units.shape[0], memory.shape[0]
    step = 128
    return pl.pallas_call(
        logits_kernel,
        grid=(rows // step,),
        in_specs=[
            pl.BlockSpec((step, KEY), lambda at: (at, 0)),
            pl.BlockSpec((columns, KEY), lambda at: (0, 0)),
        ],
        out_specs=pl.BlockSpec((step, columns), lambda at: (at, 0)),
        out_shape=shape(rows, columns),
        compiler_params=params(12),
        cost_estimate=pl.CostEstimate(
            flops=2 * rows * columns * KEY, bytes_accessed=2 * rows * columns, transcendentals=0
        ),
        name="logits",
    )(units, memory)


def queue_call(place, near, far, memory):
    return pl.pallas_call(
        queue_kernel,
        in_specs=[SMEM, ANY, ANY, ANY],
        out_specs=VMEM,
        out_shape=shape(*memory.shape),
        scratch_shapes=[
            scratch(2 * memory.shape[0] + 4 * IMAGES * IMAGES + ALIGN, KEY),
            scratch(*memory.shape),
            dma(5),
        ],
        compiler_params=params(32),
        name="queue",
    )(place, near.reshape(-1, KEY), far.reshape(-1, KEY), memory)


def per_device(
    activations, shuffle, pointer, conv_reduce, conv_spatial, conv_expand, key_head, queries, negative_memory
):
    group, member = lax.axis_index("group"), lax.axis_index("member")
    members = lax.axis_size("member")
    slots = negative_memory.shape[0]
    total_slots = slots * members
    batch = shuffle.shape[0]
    offset = jnp.mod(member * slots - pointer[0], total_slots)
    wrapped = jnp.where(offset > total_slots - slots, offset - total_slots, batch)
    start = slots + jnp.where(offset < batch, offset, wrapped)
    place = jnp.stack([group, member, group % 2, start]).astype(jnp.int32)

    x = activations.transpose(1, 2, 0, 3).reshape(ROWS, OUT)
    spatial_weight = conv_spatial.reshape(3, 3 * MID, MID)
    table = shuffle.reshape(batch // KEY, KEY)
    x, spatial_weight, expand_weight, delta, mean, select, message = reduce_call(
        place, x, conv_reduce, table, queries, spatial_weight, conv_expand
    )
    received = lax.all_to_all(message, "member", split_axis=0, concat_axis=0, tiled=True)
    moments, units = block_call(received, spatial_weight, expand_weight)
    returned = lax.all_to_all(moments, "member", split_axis=0, concat_axis=0, tiled=True)
    copies, similarity = home_call(
        returned, select, mean, delta, spatial_weight, expand_weight, x, key_head, queries, 2 * members
    )
    copies, units = lax.optimization_barrier((copies, units))
    logits = logits_call(units, negative_memory)
    same_core = [[g * members + m for g in (core, core + 2) for m in range(members)] for core in (0, 1)]
    near = lax.all_to_all(
        copies, ("group", "member"), split_axis=0, concat_axis=0, tiled=True, axis_index_groups=same_core
    )
    near, logits = lax.optimization_barrier((near, logits))
    far = lax.ppermute(near, "group", [(0, 1), (1, 0), (2, 3), (3, 2)])
    new_queue = queue_call(place, near, far, negative_memory)
    return logits, similarity.reshape(IMAGES), new_queue


def solution(mesh):
    placed = (
        P(("group", "member"), None, None, None),
        P(),
        P(),
        P(),
        P(),
        P(),
        P(),
        P(("group", "member"), None),
        P("member", None),
    )
    return jax.shard_map(
        per_device,
        mesh=mesh,
        in_specs=placed,
        out_specs=(P("group", "member"), P(("group", "member")), P("member", None)),
        check_vma=False,
    )
```

```python
import jax
import jax.numpy as jnp
from jax import lax
from jax.experimental import pallas as pl
from jax.experimental.pallas import tpu as pltpu
from jax.sharding import PartitionSpec as P

norm_eps = 1e-05
unit_eps = 1e-06
sharpness_divisor = 0.2

IMAGES = 32
SIDE = 7
POSITIONS = SIDE * SIDE
ROW = SIDE * IMAGES
ROWS = POSITIONS * IMAGES
MID = 512
OUT = 2048
KEY = 128
SLAB = 8
SLABS = POSITIONS // SLAB
SIZE = SLAB * IMAGES
LAST = SLABS * MID
QUERIES = LAST + KEY
MESSAGE = QUERIES + MID
MOMENTS = 6 * KEY
MIB = 1 << 20
f32 = jnp.float32
bf16 = jnp.bfloat16


def iota(shape, dim):
    return lax.broadcasted_iota(jnp.int32, shape, dim)


def dot(a, b):
    return jnp.dot(a, b, preferred_element_type=f32)


def dot_tn(a, b):
    return lax.dot_general(a, b, (((0,), (0,)), ((), ())), preferred_element_type=f32)


def dot_nt(a, b):
    return lax.dot_general(a, b, (((1,), (1,)), ((), ())), preferred_element_type=f32)


def spread_select(select):
    left = (iota((SIZE, IMAGES), 0) // SLAB == iota((SIZE, IMAGES), 1)).astype(bf16)
    right = (iota((IMAGES, SIZE), 0) == iota((IMAGES, SIZE), 1) % IMAGES).astype(bf16)
    spread = dot(dot(left, select).astype(bf16), right)
    same = iota((SIZE, SIZE), 0) % SLAB == iota((SIZE, SIZE), 1) // IMAGES
    return jnp.where(same, spread, 0.0).astype(bf16)


def quarters(value):
    return jnp.concatenate([value[:, k * KEY : (k + 1) * KEY] for k in range(4)], axis=0)


def whole(pieces):
    return jnp.concatenate([pieces[k] for k in range(4)], axis=1)


def split(value):
    high = value.astype(bf16).astype(f32)
    return high, value - high


def unit_of(queries):
    query_f = queries.astype(f32)
    return query_f * lax.rsqrt(jnp.sum(query_f * query_f, axis=1, keepdims=True) + unit_eps)


def start_all(pairs, sems):
    copies = [pltpu.make_async_copy(a, b, sems.at[k]) for k, (a, b) in enumerate(pairs)]
    for copy in copies:
        copy.start()
    return copies


def peer_selector(place_ref, table):
    per_row = KEY // IMAGES
    block_rows = table[pl.ds(pl.multiple_of(place_ref[0] * SLAB, SLAB), SLAB), :]
    local = block_rows - (place_ref[0] * (IMAGES * IMAGES) + place_ref[1] * IMAGES)
    mine = jnp.logical_and(local >= 0, local < IMAGES)
    found = jnp.where(mine, local, 0).astype(f32).astype(bf16)
    by_block = (iota((IMAGES, SLAB), 0) // per_row == iota((IMAGES, SLAB), 1)).astype(bf16)
    inside = iota((IMAGES, KEY), 1) // IMAGES == iota((IMAGES, KEY), 0) % per_row
    chosen = jnp.sum(jnp.where(inside, dot(by_block, found), 0.0), axis=1, keepdims=True)
    return (chosen == iota((IMAGES, IMAGES), 1).astype(f32)).astype(bf16)


def reduce_kernel(
    place_ref, x_hbm, weight_hbm, table_hbm, query_hbm, spatial_hbm, expand_hbm,
    x, spatial_weight, expand_weight, delta, mean_ref, select_ref, message,
    weight, table, query, sems,
):
    map_rows = [pl.ds(y * ROW, ROW) for y in range(SIDE)]
    weight_rows = [pl.ds(k * MID, MID) for k in range(OUT // MID)]
    loads = start_all(
        [(table_hbm, table), (query_hbm, query)]
        + [(weight_hbm.at[rows, :], weight.at[rows, :]) for rows in weight_rows]
        + [(x_hbm.at[rows, :], x.at[rows, :]) for rows in map_rows]
        + [(spatial_hbm.at[k], spatial_weight.at[k]) for k in range(3)]
        + [(expand_hbm, expand_weight)],
        sems,
    )

    loads[0].wait()
    loads[1].wait()
    select = peer_selector(place_ref, table)
    select_ref[...] = select
    mover = spread_select(select)
    unit = unit_of(query[...])
    unit = jnp.concatenate([unit[SLAB * k : SLAB * (k + 1)] for k in range(4)], axis=1)
    message[:, :, pl.ds(QUERIES, MID)] = jnp.broadcast_to(unit[None], (IMAGES, SLAB, MID)).astype(bf16)
    for copy in loads[2:6]:
        copy.wait()
    done = [0]
    parts = []

    def finish(y):
        delta[map_rows[y], :] = (parts[y] - mean_f[None]).reshape(ROW, MID).astype(bf16)
        while (done[0] + 1) * SLAB <= (y + 1) * SIDE:
            moved = dot(mover, delta[pl.ds(done[0] * SIZE, SIZE), :]).reshape(IMAGES, SLAB, MID)
            message[:, :, pl.ds(done[0] * MID, MID)] = moved.astype(bf16)
            done[0] += 1

    for y in range(SIDE):
        for k in {0: [0], 1: [1, 2, 3], 4: [4, 5, 6]}.get(y, ()):
            loads[6 + k].wait()
        part = dot(x[map_rows[y], :], weight[...]).reshape(SIDE, IMAGES, MID)
        if y == 0:
            mean = (jnp.sum(part, axis=0) * (1.0 / SIDE)).astype(bf16)
            mean_f = mean.astype(f32)
            mean_ref[...] = mean
        if y > 0:
            finish(y - 1)
        parts.append(part)
    finish(SIDE - 1)
    last = jnp.concatenate([quarters(delta[pl.ds(SLABS * SIZE, IMAGES), :]), quarters(mean)], axis=0)
    message[:, :, pl.ds(LAST, KEY)] = dot(mover, last).reshape(IMAGES, SLAB, KEY).astype(bf16)
    for copy in loads[6 + SIDE :]:
        copy.wait()


def store_windows(windows, reduced, y):
    edge = jnp.zeros((IMAGES, MID), bf16)
    at = (y + 1) * ROW
    windows[pl.ds(at, IMAGES), pl.ds(0, MID)] = edge
    windows[pl.ds(at + IMAGES, ROW - IMAGES), pl.ds(0, MID)] = reduced[: ROW - IMAGES]
    windows[pl.ds(at, ROW), pl.ds(MID, MID)] = reduced
    windows[pl.ds(at, ROW - IMAGES), pl.ds(2 * MID, MID)] = reduced[IMAGES:]
    windows[pl.ds(at + ROW - IMAGES, IMAGES), pl.ds(2 * MID, MID)] = edge


def clear_border(windows):
    border = jnp.zeros((ROW, 3 * MID), bf16)
    windows[pl.ds(0, ROW), :] = border
    windows[pl.ds((SIDE + 1) * ROW, ROW), :] = border


def convolve_row(windows, spatial_weight, y):
    return dot(
        jnp.concatenate([windows[pl.ds((y + k) * ROW, ROW), :] for k in range(3)], axis=1),
        spatial_weight[...].reshape(9 * MID, MID),
    )


def fold(value):
    return jnp.sum(value.reshape(-1, IMAGES, value.shape[1]), axis=0)


def block_mean(total):
    return jnp.sum(total, axis=0, keepdims=True) * (1.0 / ROWS)


def block_kernel(received, spatial_weight, expand_weight, moments, units, values, windows, square_sums):
    clear_border(windows)
    row, column = iota((SIZE, SIZE), 0), iota((SIZE, SIZE), 1)
    mover = jnp.logical_and(row % IMAGES == column // SLAB, row // IMAGES == column % SLAB).astype(bf16)

    tail = dot(mover, received[:, :, pl.ds(LAST, KEY)].reshape(SIZE, KEY)).reshape(SLAB, IMAGES, KEY)
    mean = whole(tail[4:])
    shift = jnp.sum(mean, axis=0, keepdims=True) * (1.0 / IMAGES)
    away = mean - shift
    last = whole(tail[:4]) + away
    values[pl.ds(SLABS * SIZE, IMAGES), :] = last
    total, squares = last, last * last
    for slab in range(SLABS):
        moved = dot(mover, received[:, :, pl.ds(slab * MID, MID)].reshape(SIZE, MID))
        moved = (moved.reshape(SLAB, IMAGES, MID) + away[None]).reshape(SIZE, MID)
        values[pl.ds(slab * SIZE, SIZE), :] = moved
        total = total + fold(moved)
        squares = squares + fold(moved * moved)
    offset1 = block_mean(total)
    center1 = shift + offset1
    scale1 = lax.rsqrt(block_mean(squares) - offset1 * offset1 + norm_eps).astype(bf16).astype(f32)
    queries = received[:, :, pl.ds(QUERIES, MID)].astype(f32)
    queries = jnp.concatenate([queries[:, None, :, k * KEY : (k + 1) * KEY] for k in range(4)], axis=1)
    units[...] = queries.reshape(IMAGES * IMAGES, KEY).astype(bf16)

    def normalize(y):
        reduced = jnp.maximum((values[pl.ds(y * ROW, ROW), :] - offset1) * scale1, 0.0)
        store_windows(windows, reduced.astype(bf16), y)

    normalize(0)
    total = squares = jnp.zeros((IMAGES, MID), f32)
    for y in range(SIDE):
        if y + 1 < SIDE:
            normalize(y + 1)
        second = convolve_row(windows, spatial_weight, y)
        values[pl.ds(y * ROW, ROW), :] = second
        total = total + fold(second)
        squares = squares + fold(second * second)
    center2 = block_mean(total)
    scale2 = lax.rsqrt(block_mean(squares) - center2 * center2 + norm_eps).astype(bf16).astype(f32)
    total = jnp.zeros((IMAGES, MID), f32)
    parts = range(OUT // MID)
    for y in range(SIDE):
        kept = jnp.maximum((values[pl.ds(y * ROW, ROW), :] - center2) * scale2, 0.0).astype(bf16)
        total = total + fold(kept.astype(f32))
        for part in parts:
            third = dot(kept, expand_weight[:, pl.ds(part * MID, MID)])
            square = fold(third * third)
            square_sums[part] = square if y == 0 else square_sums[part] + square
    mean_high, mean_low = split(block_mean(total))
    scale3 = []
    for part in parts:
        weight = expand_weight[:, pl.ds(part * MID, MID)]
        center3 = dot(mean_high.astype(bf16), weight) + dot(mean_low.astype(bf16), weight)
        scale3.append(lax.rsqrt(block_mean(square_sums[part]) - center3 * center3 + norm_eps))

    vectors = [*split(center1), *split(center2), mean_high, mean_low, scale1, scale2, *scale3]
    vectors = [quarters(vector) for vector in vectors]
    tiles = [jnp.concatenate(vectors[k : k + 2], axis=0) for k in range(0, 12, 2)]
    packed = jnp.concatenate(tiles, axis=1)
    moments[...] = jnp.broadcast_to(packed[None], (IMAGES, SLAB, MOMENTS)).astype(bf16)


def home_kernel(
    received, select, mean, delta, spatial_weight, expand_weight, x, head, query,
    keys, similarity_ref, windows, spatial, pooled,
):
    clear_border(windows)
    stats = dot_tn(spread_select(select[...]), received[...].reshape(SIZE, MOMENTS))
    stats = stats.reshape(SLAB, IMAGES, MOMENTS)
    vectors = []
    for k in range(12):
        half, lanes = 4 * (k % 2), k // 2 * KEY
        vectors.append(whole([stats[half + q, :, lanes : lanes + KEY] for q in range(4)]))
    offset1 = mean[...].astype(f32) - (vectors[0] + vectors[1])
    center2 = vectors[2] + vectors[3]
    mean_high, mean_low = vectors[4].astype(bf16), vectors[5].astype(bf16)
    scale1, scale2 = vectors[6], vectors[7]

    def normalize(y):
        away = delta[pl.ds(y * ROW, ROW), :].astype(f32).reshape(SIDE, IMAGES, MID)
        reduced = jnp.maximum((away + offset1[None]) * scale1[None], 0.0)
        store_windows(windows, reduced.reshape(ROW, MID).astype(bf16), y)

    normalize(0)

    for y in range(SIDE):
        if y + 1 < SIDE:
            normalize(y + 1)
        second = convolve_row(windows, spatial_weight, y).reshape(SIDE, IMAGES, MID)
        kept = jnp.maximum((second - center2[None]) * scale2[None], 0.0)
        spatial[pl.ds(y * ROW, ROW), :] = kept.reshape(ROW, MID).astype(bf16)

    for part in range(OUT // MID):
        columns = pl.ds(part * MID, MID)
        weight = expand_weight[:, columns]
        center3 = dot(mean_high, weight) + dot(mean_low, weight)
        scale3 = vectors[8 + part]
        total = jnp.zeros((IMAGES, MID), f32)
        for y in range(SIDE):
            rows = pl.ds(y * ROW, ROW)
            third = dot(spatial[rows, :], weight).reshape(SIDE, IMAGES, MID)
            kept = x[rows, columns].astype(f32).reshape(SIDE, IMAGES, MID)
            merged = jnp.maximum((third - center3[None]) * scale3[None] + kept, 0.0)
            total = total + jnp.sum(merged, axis=0)
        pooled[:, columns] = (total * (1.0 / POSITIONS)).astype(bf16)
    projected = dot(pooled[...], head[...])
    key = projected * lax.rsqrt(jnp.sum(projected * projected, axis=1, keepdims=True) + unit_eps)
    key = key.astype(bf16)
    keys[...] = jnp.broadcast_to(key[None], keys.shape)
    unit = unit_of(query[...]).astype(bf16)
    pairs = dot_nt(unit, key)
    own = iota((IMAGES, IMAGES), 0) == iota((IMAGES, IMAGES), 1)
    similarity_ref[...] = jnp.sum(jnp.where(own, pairs, 0.0), axis=0, keepdims=True) / sharpness_divisor


def logits_kernel(units_ref, memory_ref, out_ref):
    out_ref[...] = (dot_nt(units_ref[...], memory_ref[...]) * (1.0 / sharpness_divisor)).astype(bf16)


def queue_kernel(place_ref, near_hbm, far_hbm, memory_hbm, out_ref, padded, memory, sems):
    slots = memory.shape[0]
    batch = 4 * IMAGES * IMAGES
    half = IMAGES * IMAGES
    core = place_ref[2]
    start = place_ref[3]
    pairs = [(memory_hbm, memory)]
    for high in range(2):
        for ref, which in ((near_hbm, core), (far_hbm, 1 - core)):
            at = pl.multiple_of(slots + (2 * high + which) * half, half)
            pairs.append((ref.at[pl.ds(high * half, half), :], padded.at[pl.ds(at, half), :]))
    loads = start_all(pairs, sems)
    edge = jnp.zeros((slots, KEY), bf16)
    padded[pl.ds(0, slots), :] = edge
    padded[pl.ds(slots + batch, slots), :] = edge
    padded[pl.ds(2 * slots + batch, ALIGN), :] = edge[:ALIGN]
    base = start // ALIGN * ALIGN
    inner = start - base
    pick = (iota((TILE, TILE + ALIGN), 1) == iota((TILE, TILE + ALIGN), 0) + inner).astype(bf16)
    for copy in loads:
        copy.wait()
    for part in range(slots // TILE):
        rows = padded[pl.ds(pl.multiple_of(base + part * TILE, ALIGN), TILE + ALIGN), :]
        fresh = dot(pick, rows)
        index = start - slots + part * TILE + iota((TILE, KEY), 0)
        inside = jnp.logical_and(index >= 0, index < batch)
        old = memory[pl.ds(part * TILE, TILE), :].astype(f32)
        out_ref[pl.ds(part * TILE, TILE), :] = jnp.where(inside, fresh, old).astype(bf16)


ALIGN = 16
TILE = 256


def params(mib):
    return pltpu.CompilerParams(vmem_limit_bytes=mib * MIB)


VMEM = pl.BlockSpec(memory_space=pltpu.VMEM)
SMEM = pl.BlockSpec(memory_space=pltpu.SMEM)
ANY = pl.BlockSpec(memory_space=pl.ANY)
HBM = pl.BlockSpec(memory_space=pltpu.HBM)


def shape(*dims, dtype=bf16):
    return jax.ShapeDtypeStruct(dims, dtype)


def scratch(*dims, dtype=bf16):
    return pltpu.VMEM(dims, dtype)


def dma(count):
    return pltpu.SemaphoreType.DMA((count,))


def in_hbm(*arrays):
    return [pltpu.with_memory_space_constraint(array, pltpu.HBM) for array in arrays]


def in_vmem(*arrays):
    return [pltpu.with_memory_space_constraint(array, pltpu.VMEM) for array in arrays]


def reduce_call(place, x, conv_reduce, table, queries, conv_spatial, conv_expand):
    return pl.pallas_call(
        reduce_kernel,
        in_specs=[SMEM] + [HBM] * 6,
        out_specs=[VMEM] * 7,
        out_shape=[
            scratch(ROWS, OUT),
            scratch(*conv_spatial.shape),
            scratch(MID, OUT),
            scratch(ROWS, MID),
            scratch(IMAGES, MID),
            scratch(IMAGES, IMAGES),
            scratch(IMAGES, SLAB, MESSAGE),
        ],
        scratch_shapes=[
            scratch(OUT, MID),
            scratch(*table.shape, dtype=jnp.int32),
            scratch(IMAGES, KEY),
            dma(10 + SIDE),
        ],
        compiler_params=params(24),
        name="reduce",
    )(place, *in_hbm(x, conv_reduce, table, queries, conv_spatial, conv_expand))


def block_call(received, spatial_weight, expand_weight):
    return pl.pallas_call(
        block_kernel,
        in_specs=[VMEM] * 3,
        out_specs=[VMEM, VMEM],
        out_shape=[scratch(IMAGES, SLAB, MOMENTS), scratch(IMAGES * IMAGES, KEY)],
        scratch_shapes=[
            scratch(ROWS, MID, dtype=f32),
            scratch(ROWS + 2 * ROW, 3 * MID),
            scratch(OUT // MID, IMAGES, MID, dtype=f32),
        ],
        compiler_params=params(30),
        name="block",
    )(*in_vmem(received, spatial_weight, expand_weight))


def home_call(received, select, mean, delta, spatial_weight, expand_weight, x, key_head, queries, copies):
    return pl.pallas_call(
        home_kernel,
        in_specs=[VMEM] * 9,
        out_specs=[VMEM, VMEM],
        out_shape=[scratch(copies, IMAGES, KEY), shape(1, IMAGES, dtype=f32)],
        scratch_shapes=[
            scratch(ROWS + 2 * ROW, 3 * MID),
            scratch(ROWS, MID),
            scratch(IMAGES, OUT),
        ],
        compiler_params=params(30),
        name="home",
    )(*in_vmem(received, select, mean, delta, spatial_weight, expand_weight, x), key_head, queries)


def logits_call(units, memory):
    rows, columns = units.shape[0], memory.shape[0]
    step = 128
    return pl.pallas_call(
        logits_kernel,
        grid=(rows // step,),
        in_specs=[
            pl.BlockSpec((step, KEY), lambda at: (at, 0)),
            pl.BlockSpec((columns, KEY), lambda at: (0, 0)),
        ],
        out_specs=pl.BlockSpec((step, columns), lambda at: (at, 0)),
        out_shape=shape(rows, columns),
        compiler_params=params(12),
        cost_estimate=pl.CostEstimate(
            flops=2 * rows * columns * KEY, bytes_accessed=2 * rows * columns, transcendentals=0
        ),
        name="logits",
    )(units, memory)


def queue_call(place, near, far, memory):
    return pl.pallas_call(
        queue_kernel,
        in_specs=[SMEM, ANY, ANY, ANY],
        out_specs=VMEM,
        out_shape=shape(*memory.shape),
        scratch_shapes=[
            scratch(2 * memory.shape[0] + 4 * IMAGES * IMAGES + ALIGN, KEY),
            scratch(*memory.shape),
            dma(5),
        ],
        compiler_params=params(32),
        name="queue",
    )(place, near.reshape(-1, KEY), far.reshape(-1, KEY), memory)


def per_device(
    activations, shuffle, pointer, conv_reduce, conv_spatial, conv_expand, key_head, queries, negative_memory
):
    group, member = lax.axis_index("group"), lax.axis_index("member")
    members = lax.axis_size("member")
    slots = negative_memory.shape[0]
    total_slots = slots * members
    batch = shuffle.shape[0]
    offset = jnp.mod(member * slots - pointer[0], total_slots)
    wrapped = jnp.where(offset > total_slots - slots, offset - total_slots, batch)
    start = slots + jnp.where(offset < batch, offset, wrapped)
    place = jnp.stack([group, member, group % 2, start]).astype(jnp.int32)

    x = activations.transpose(1, 2, 0, 3).reshape(ROWS, OUT)
    spatial_weight = conv_spatial.reshape(3, 3 * MID, MID)
    table = shuffle.reshape(batch // KEY, KEY)
    x, spatial_weight, expand_weight, delta, mean, select, message = reduce_call(
        place, x, conv_reduce, table, queries, spatial_weight, conv_expand
    )
    received = lax.all_to_all(message, "member", split_axis=0, concat_axis=0, tiled=True)
    moments, units = block_call(received, spatial_weight, expand_weight)
    returned = lax.all_to_all(moments, "member", split_axis=0, concat_axis=0, tiled=True)
    copies, similarity = home_call(
        returned, select, mean, delta, spatial_weight, expand_weight, x, key_head, queries, 2 * members
    )
    copies, units = lax.optimization_barrier((copies, units))
    logits = logits_call(units, negative_memory)
    same_core = [[g * members + m for g in (core, core + 2) for m in range(members)] for core in (0, 1)]
    near = lax.all_to_all(
        copies, ("group", "member"), split_axis=0, concat_axis=0, tiled=True, axis_index_groups=same_core
    )
    near, logits = lax.optimization_barrier((near, logits))
    far = lax.ppermute(near, "group", [(0, 1), (1, 0), (2, 3), (3, 2)])
    new_queue = queue_call(place, near, far, negative_memory)
    return logits, similarity.reshape(IMAGES), new_queue


def solution(mesh):
    placed = (
        P(("group", "member"), None, None, None),
        P(),
        P(),
        P(),
        P(),
        P(),
        P(),
        P(("group", "member"), None),
        P("member", None),
    )
    return jax.shard_map(
        per_device,
        mesh=mesh,
        in_specs=placed,
        out_specs=(P("group", "member"), P(("group", "member")), P("member", None)),
        check_vma=False,
    )
```

```python
import jax
import jax.numpy as jnp
from jax import lax
from jax.experimental import pallas as pl
from jax.experimental.pallas import tpu as pltpu
from jax.sharding import PartitionSpec as P

norm_eps = 1e-05
unit_eps = 1e-06
sharpness_divisor = 0.2

IMAGES = 32
SIDE = 7
POSITIONS = SIDE * SIDE
ROW = SIDE * IMAGES
ROWS = POSITIONS * IMAGES
MID = 512
OUT = 2048
KEY = 128
SLAB = 8
SLABS = POSITIONS // SLAB
SIZE = SLAB * IMAGES
LAST = SLABS * MID
QUERIES = LAST + KEY
MESSAGE = QUERIES + MID
MOMENTS = 6 * KEY
MIB = 1 << 20
f32 = jnp.float32
bf16 = jnp.bfloat16


def iota(shape, dim):
    return lax.broadcasted_iota(jnp.int32, shape, dim)


def dot(a, b):
    return jnp.dot(a, b, preferred_element_type=f32)


def dot_tn(a, b):
    return lax.dot_general(a, b, (((0,), (0,)), ((), ())), preferred_element_type=f32)


def dot_nt(a, b):
    return lax.dot_general(a, b, (((1,), (1,)), ((), ())), preferred_element_type=f32)


def spread_select(select):
    left = (iota((SIZE, IMAGES), 0) // SLAB == iota((SIZE, IMAGES), 1)).astype(bf16)
    right = (iota((IMAGES, SIZE), 0) == iota((IMAGES, SIZE), 1) % IMAGES).astype(bf16)
    spread = dot(dot(left, select).astype(bf16), right)
    same = iota((SIZE, SIZE), 0) % SLAB == iota((SIZE, SIZE), 1) // IMAGES
    return jnp.where(same, spread, 0.0).astype(bf16)


def quarters(value):
    return jnp.concatenate([value[:, k * KEY : (k + 1) * KEY] for k in range(4)], axis=0)


def whole(pieces):
    return jnp.concatenate([pieces[k] for k in range(4)], axis=1)


def split(value):
    high = value.astype(bf16).astype(f32)
    return high, value - high


def unit_of(queries):
    query_f = queries.astype(f32)
    return query_f * lax.rsqrt(jnp.sum(query_f * query_f, axis=1, keepdims=True) + unit_eps)


def start_all(pairs, sems):
    copies = [pltpu.make_async_copy(a, b, sems.at[k]) for k, (a, b) in enumerate(pairs)]
    for copy in copies:
        copy.start()
    return copies


def peer_selector(place_ref, table):
    per_row = KEY // IMAGES
    block_rows = table[pl.ds(pl.multiple_of(place_ref[0] * SLAB, SLAB), SLAB), :]
    local = block_rows - (place_ref[0] * (IMAGES * IMAGES) + place_ref[1] * IMAGES)
    mine = jnp.logical_and(local >= 0, local < IMAGES)
    found = jnp.where(mine, local, 0).astype(f32).astype(bf16)
    by_block = (iota((IMAGES, SLAB), 0) // per_row == iota((IMAGES, SLAB), 1)).astype(bf16)
    inside = iota((IMAGES, KEY), 1) // IMAGES == iota((IMAGES, KEY), 0) % per_row
    chosen = jnp.sum(jnp.where(inside, dot(by_block, found), 0.0), axis=1, keepdims=True)
    return (chosen == iota((IMAGES, IMAGES), 1).astype(f32)).astype(bf16)


WAITS = {0: (0,), 1: (1, 2), 3: (3, 4, 5, 6)}


def reduce_kernel(
    place_ref, x_hbm, weight_hbm, table_hbm, query_hbm, spatial_hbm, expand_hbm,
    x, spatial_weight, expand_weight, delta, mean_ref, back_ref, message,
    weight, table, query, sems,
):
    map_rows = [pl.ds(y * ROW, ROW) for y in range(SIDE)]
    weight_rows = [pl.ds(k * MID, MID) for k in range(OUT // MID)]
    loads = start_all(
        [(table_hbm, table), (query_hbm, query)]
        + [(weight_hbm.at[rows, :], weight.at[rows, :]) for rows in weight_rows]
        + [(x_hbm.at[rows, :], x.at[rows, :]) for rows in map_rows]
        + [(spatial_hbm.at[k], spatial_weight.at[k]) for k in range(3)]
        + [(expand_hbm, expand_weight)],
        sems,
    )

    loads[0].wait()
    loads[1].wait()
    mover = spread_select(peer_selector(place_ref, table))
    same = (iota((SIZE, SIZE), 0) == iota((SIZE, SIZE), 1)).astype(bf16)
    back_ref[...] = dot_tn(mover, same).astype(bf16)
    unit = unit_of(query[...])
    unit = jnp.concatenate([unit[SLAB * k : SLAB * (k + 1)] for k in range(4)], axis=1)
    message[:, :, pl.ds(QUERIES, MID)] = jnp.broadcast_to(unit[None], (IMAGES, SLAB, MID)).astype(bf16)
    for copy in loads[2:6]:
        copy.wait()
    done = [0]
    parts = []

    def finish(y):
        delta[map_rows[y], :] = (parts[y] - mean_f[None]).reshape(ROW, MID).astype(bf16)
        while (done[0] + 1) * SLAB <= (y + 1) * SIDE:
            moved = dot(mover, delta[pl.ds(done[0] * SIZE, SIZE), :]).reshape(IMAGES, SLAB, MID)
            message[:, :, pl.ds(done[0] * MID, MID)] = moved.astype(bf16)
            done[0] += 1

    for y in range(SIDE):
        for k in WAITS.get(y, ()):
            loads[6 + k].wait()
        part = dot(x[map_rows[y], :], weight[...]).reshape(SIDE, IMAGES, MID)
        if y == 0:
            mean = (jnp.sum(part, axis=0) * (1.0 / SIDE)).astype(bf16)
            mean_f = mean.astype(f32)
            mean_ref[...] = mean
        if y > 0:
            finish(y - 1)
        parts.append(part)
    finish(SIDE - 1)
    last = jnp.concatenate([quarters(delta[pl.ds(SLABS * SIZE, IMAGES), :]), quarters(mean)], axis=0)
    message[:, :, pl.ds(LAST, KEY)] = dot(mover, last).reshape(IMAGES, SLAB, KEY).astype(bf16)
    for copy in loads[6 + SIDE :]:
        copy.wait()


def store_windows(windows, reduced, y):
    edge = jnp.zeros((IMAGES, MID), bf16)
    at = (y + 1) * ROW
    windows[pl.ds(at, IMAGES), pl.ds(0, MID)] = edge
    windows[pl.ds(at + IMAGES, ROW - IMAGES), pl.ds(0, MID)] = reduced[: ROW - IMAGES]
    windows[pl.ds(at, ROW), pl.ds(MID, MID)] = reduced
    windows[pl.ds(at, ROW - IMAGES), pl.ds(2 * MID, MID)] = reduced[IMAGES:]
    windows[pl.ds(at + ROW - IMAGES, IMAGES), pl.ds(2 * MID, MID)] = edge


def clear_border(windows):
    border = jnp.zeros((ROW, 3 * MID), bf16)
    windows[pl.ds(0, ROW), :] = border
    windows[pl.ds((SIDE + 1) * ROW, ROW), :] = border


def convolve_row(windows, spatial_weight, y):
    return dot(
        jnp.concatenate([windows[pl.ds((y + k) * ROW, ROW), :] for k in range(3)], axis=1),
        spatial_weight[...].reshape(9 * MID, MID),
    )


def fold(value):
    return jnp.sum(value.reshape(-1, IMAGES, value.shape[1]), axis=0)


def block_mean(total):
    return jnp.sum(total, axis=0, keepdims=True) * (1.0 / ROWS)


def block_kernel(received, spatial_weight, expand_weight, moments, units, values, windows, square_sums):
    clear_border(windows)
    row, column = iota((SIZE, SIZE), 0), iota((SIZE, SIZE), 1)
    mover = jnp.logical_and(row % IMAGES == column // SLAB, row // IMAGES == column % SLAB).astype(bf16)

    tail = dot(mover, received[:, :, pl.ds(LAST, KEY)].reshape(SIZE, KEY)).reshape(SLAB, IMAGES, KEY)
    mean = whole(tail[4:])
    shift = jnp.sum(mean, axis=0, keepdims=True) * (1.0 / IMAGES)
    away = mean - shift
    last = whole(tail[:4]) + away
    values[pl.ds(SLABS * SIZE, IMAGES), :] = last
    total, squares = last, last * last
    for slab in range(SLABS):
        moved = dot(mover, received[:, :, pl.ds(slab * MID, MID)].reshape(SIZE, MID))
        moved = (moved.reshape(SLAB, IMAGES, MID) + away[None]).reshape(SIZE, MID)
        values[pl.ds(slab * SIZE, SIZE), :] = moved
        total = total + fold(moved)
        squares = squares + fold(moved * moved)
    offset1 = block_mean(total)
    center1 = shift + offset1
    scale1 = lax.rsqrt(block_mean(squares) - offset1 * offset1 + norm_eps).astype(bf16).astype(f32)
    queries = received[:, :, pl.ds(QUERIES, MID)].astype(f32)
    queries = jnp.concatenate([queries[:, None, :, k * KEY : (k + 1) * KEY] for k in range(4)], axis=1)
    units[...] = queries.reshape(IMAGES * IMAGES, KEY).astype(bf16)

    def normalize(y):
        reduced = jnp.maximum((values[pl.ds(y * ROW, ROW), :] - offset1) * scale1, 0.0)
        store_windows(windows, reduced.astype(bf16), y)

    normalize(0)
    total = squares = jnp.zeros((IMAGES, MID), f32)
    for y in range(SIDE):
        if y + 1 < SIDE:
            normalize(y + 1)
        second = convolve_row(windows, spatial_weight, y)
        values[pl.ds(y * ROW, ROW), :] = second
        total = total + fold(second)
        squares = squares + fold(second * second)
    center2 = block_mean(total)
    scale2 = lax.rsqrt(block_mean(squares) - center2 * center2 + norm_eps).astype(bf16).astype(f32)
    total = jnp.zeros((IMAGES, MID), f32)
    parts = range(OUT // MID)
    for y in range(SIDE):
        kept = jnp.maximum((values[pl.ds(y * ROW, ROW), :] - center2) * scale2, 0.0).astype(bf16)
        total = total + fold(kept.astype(f32))
        for part in parts:
            third = dot(kept, expand_weight[:, pl.ds(part * MID, MID)])
            square = fold(third * third)
            square_sums[part] = square if y == 0 else square_sums[part] + square
    mean_high, mean_low = split(block_mean(total))
    scale3 = []
    for part in parts:
        weight = expand_weight[:, pl.ds(part * MID, MID)]
        center3 = dot(mean_high.astype(bf16), weight) + dot(mean_low.astype(bf16), weight)
        scale3.append(lax.rsqrt(block_mean(square_sums[part]) - center3 * center3 + norm_eps))

    vectors = [*split(center1), *split(center2), mean_high, mean_low, scale1, scale2, *scale3]
    vectors = [quarters(vector) for vector in vectors]
    tiles = [jnp.concatenate(vectors[k : k + 2], axis=0) for k in range(0, 12, 2)]
    packed = jnp.concatenate(tiles, axis=1)
    moments[...] = jnp.broadcast_to(packed[None], (IMAGES, SLAB, MOMENTS)).astype(bf16)


def home_kernel(
    received, back, mean, delta, spatial_weight, expand_weight, x, head,
    keys, windows, spatial, pooled,
):
    clear_border(windows)
    stats = dot(back[...], received[...].reshape(SIZE, MOMENTS))
    stats = stats.reshape(SLAB, IMAGES, MOMENTS)
    vectors = []
    for k in range(12):
        half, lanes = 4 * (k % 2), k // 2 * KEY
        vectors.append(whole([stats[half + q, :, lanes : lanes + KEY] for q in range(4)]))
    offset1 = mean[...].astype(f32) - (vectors[0] + vectors[1])
    center2 = vectors[2] + vectors[3]
    mean_high, mean_low = vectors[4].astype(bf16), vectors[5].astype(bf16)
    scale1, scale2 = vectors[6], vectors[7]

    def normalize(y):
        away = delta[pl.ds(y * ROW, ROW), :].astype(f32).reshape(SIDE, IMAGES, MID)
        reduced = jnp.maximum((away + offset1[None]) * scale1[None], 0.0)
        store_windows(windows, reduced.reshape(ROW, MID).astype(bf16), y)

    normalize(0)

    for y in range(SIDE):
        if y + 1 < SIDE:
            normalize(y + 1)
        second = convolve_row(windows, spatial_weight, y).reshape(SIDE, IMAGES, MID)
        kept = jnp.maximum((second - center2[None]) * scale2[None], 0.0)
        spatial[pl.ds(y * ROW, ROW), :] = kept.reshape(ROW, MID).astype(bf16)

    for part in range(OUT // MID):
        columns = pl.ds(part * MID, MID)
        weight = expand_weight[:, columns]
        center3 = dot(mean_high, weight) + dot(mean_low, weight)
        scale3 = vectors[8 + part]
        total = jnp.zeros((IMAGES, MID), f32)
        for y in range(SIDE):
            rows = pl.ds(y * ROW, ROW)
            third = dot(spatial[rows, :], weight).reshape(SIDE, IMAGES, MID)
            kept = x[rows, columns].astype(f32).reshape(SIDE, IMAGES, MID)
            merged = jnp.maximum((third - center3[None]) * scale3[None] + kept, 0.0)
            total = total + jnp.sum(merged, axis=0)
        pooled[:, columns] = (total * (1.0 / POSITIONS)).astype(bf16)
    projected = dot(pooled[...], head[...])
    key = projected * lax.rsqrt(jnp.sum(projected * projected, axis=1, keepdims=True) + unit_eps)
    key = key.astype(bf16)
    keys[...] = jnp.broadcast_to(key[None], keys.shape)


def logits_kernel(units_ref, memory_ref, out_ref):
    out_ref[...] = (dot_nt(units_ref[...], memory_ref[...]) * (1.0 / sharpness_divisor)).astype(bf16)


def queue_kernel(place_ref, near_ref, far_ref, memory, out_hbm, padded, out_ref, sems):
    slots = memory.shape[0]
    batch = 4 * IMAGES * IMAGES
    half = IMAGES * IMAGES
    core = place_ref[2]
    start = place_ref[3]
    for high in range(2):
        for ref, which in ((near_ref, core), (far_ref, 1 - core)):
            at = pl.multiple_of(slots + (2 * high + which) * half, half)
            padded[pl.ds(at, half), :] = ref[pl.ds(high * half, half), :]
    edge = jnp.zeros((slots, KEY), bf16)
    padded[pl.ds(0, slots), :] = edge
    padded[pl.ds(slots + batch, slots), :] = edge
    padded[pl.ds(2 * slots + batch, ALIGN), :] = edge[:ALIGN]
    base = start // ALIGN * ALIGN
    inner = start - base
    pick = (iota((TILE, TILE + ALIGN), 1) == iota((TILE, TILE + ALIGN), 0) + inner).astype(bf16)
    stores = []
    for part in range(slots // TILE):
        rows = padded[pl.ds(pl.multiple_of(base + part * TILE, ALIGN), TILE + ALIGN), :]
        fresh = dot(pick, rows)
        index = start - slots + part * TILE + iota((TILE, KEY), 0)
        inside = jnp.logical_and(index >= 0, index < batch)
        old = memory[pl.ds(part * TILE, TILE), :].astype(f32)
        out_ref[pl.ds(part * TILE, TILE), :] = jnp.where(inside, fresh, old).astype(bf16)
        if (part + 1) * TILE % STORE == 0:
            rows = pl.ds((part + 1) * TILE - STORE, STORE)
            store = pltpu.make_async_copy(out_ref.at[rows, :], out_hbm.at[rows, :], sems.at[len(stores)])
            store.start()
            stores.append(store)
    for store in stores:
        store.wait()


STORE = 512
ALIGN = 16
TILE = 64


def params(mib):
    return pltpu.CompilerParams(vmem_limit_bytes=mib * MIB)


VMEM = pl.BlockSpec(memory_space=pltpu.VMEM)
SMEM = pl.BlockSpec(memory_space=pltpu.SMEM)
ANY = pl.BlockSpec(memory_space=pl.ANY)
HBM = pl.BlockSpec(memory_space=pltpu.HBM)


def shape(*dims, dtype=bf16):
    return jax.ShapeDtypeStruct(dims, dtype)


def scratch(*dims, dtype=bf16):
    return pltpu.VMEM(dims, dtype)


def dma(count):
    return pltpu.SemaphoreType.DMA((count,))


def in_hbm(*arrays):
    return [pltpu.with_memory_space_constraint(array, pltpu.HBM) for array in arrays]


def in_vmem(*arrays):
    return [pltpu.with_memory_space_constraint(array, pltpu.VMEM) for array in arrays]


def reduce_call(place, x, conv_reduce, table, queries, conv_spatial, conv_expand):
    return pl.pallas_call(
        reduce_kernel,
        in_specs=[SMEM] + [HBM] * 6,
        out_specs=[VMEM] * 7,
        out_shape=[
            scratch(ROWS, OUT),
            scratch(*conv_spatial.shape),
            scratch(MID, OUT),
            scratch(ROWS, MID),
            scratch(IMAGES, MID),
            scratch(SIZE, SIZE),
            scratch(IMAGES, SLAB, MESSAGE),
        ],
        scratch_shapes=[
            scratch(OUT, MID),
            scratch(*table.shape, dtype=jnp.int32),
            scratch(IMAGES, KEY),
            dma(10 + SIDE),
        ],
        compiler_params=params(24),
        name="reduce",
    )(place, *in_hbm(x, conv_reduce, table, queries, conv_spatial, conv_expand))


def block_call(received, spatial_weight, expand_weight):
    return pl.pallas_call(
        block_kernel,
        in_specs=[VMEM] * 3,
        out_specs=[VMEM, VMEM],
        out_shape=[scratch(IMAGES, SLAB, MOMENTS), scratch(IMAGES * IMAGES, KEY)],
        scratch_shapes=[
            scratch(ROWS, MID, dtype=f32),
            scratch(ROWS + 2 * ROW, 3 * MID),
            scratch(OUT // MID, IMAGES, MID, dtype=f32),
        ],
        compiler_params=params(30),
        name="block",
    )(*in_vmem(received, spatial_weight, expand_weight))


def home_call(received, back, mean, delta, spatial_weight, expand_weight, x, key_head, copies):
    return pl.pallas_call(
        home_kernel,
        in_specs=[VMEM] * 8,
        out_specs=VMEM,
        out_shape=scratch(copies, IMAGES, KEY),
        scratch_shapes=[
            scratch(ROWS + 2 * ROW, 3 * MID),
            scratch(ROWS, MID),
            scratch(IMAGES, OUT),
        ],
        compiler_params=params(30),
        name="home",
    )(*in_vmem(received, back, mean, delta, spatial_weight, expand_weight, x), key_head)


def logits_call(units, memory):
    rows, columns = units.shape[0], memory.shape[0]
    step = 128
    return pl.pallas_call(
        logits_kernel,
        grid=(rows // step,),
        in_specs=[
            pl.BlockSpec((step, KEY), lambda at: (at, 0)),
            pl.BlockSpec((columns, KEY), lambda at: (0, 0)),
        ],
        out_specs=pl.BlockSpec((step, columns), lambda at: (at, 0)),
        out_shape=shape(rows, columns),
        compiler_params=params(12),
        cost_estimate=pl.CostEstimate(
            flops=2 * rows * columns * KEY, bytes_accessed=2 * rows * columns, transcendentals=0
        ),
        name="logits",
    )(units, memory)


def similarity_kernel(place_ref, keys, query, similarity_ref):
    own_rows = (place_ref[0] // 2 * IMAGES + place_ref[1]) * IMAGES
    key = keys[pl.ds(pl.multiple_of(own_rows, IMAGES), IMAGES), :]
    pairs = dot_nt(unit_of(query[...]).astype(bf16), key)
    own = iota((IMAGES, IMAGES), 0) == iota((IMAGES, IMAGES), 1)
    similarity = jnp.sum(jnp.where(own, pairs, 0.0), axis=0, keepdims=True)
    similarity_ref[...] = similarity / sharpness_divisor


def similarity_call(place, near, queries):
    return pl.pallas_call(
        similarity_kernel,
        in_specs=[SMEM, VMEM, VMEM],
        out_specs=VMEM,
        out_shape=shape(1, IMAGES, dtype=f32),
        compiler_params=params(12),
        cost_estimate=pl.CostEstimate(flops=MIB, bytes_accessed=MIB, transcendentals=0),
        name="similarity",
    )(place, *in_vmem(near.reshape(-1, KEY)), queries)


def queue_call(place, near, far, memory):
    return pl.pallas_call(
        queue_kernel,
        in_specs=[SMEM, VMEM, VMEM, VMEM],
        out_specs=ANY,
        out_shape=shape(*memory.shape),
        scratch_shapes=[
            scratch(2 * memory.shape[0] + 4 * IMAGES * IMAGES + ALIGN, KEY),
            scratch(*memory.shape),
            dma(memory.shape[0] // STORE),
        ],
        compiler_params=params(32),
        name="queue",
    )(place, *in_vmem(near.reshape(-1, KEY), far.reshape(-1, KEY)), memory)


def per_device(
    activations, shuffle, pointer, conv_reduce, conv_spatial, conv_expand, key_head, queries, negative_memory
):
    group, member = lax.axis_index("group"), lax.axis_index("member")
    members = lax.axis_size("member")
    slots = negative_memory.shape[0]
    total_slots = slots * members
    batch = shuffle.shape[0]
    offset = jnp.mod(member * slots - pointer[0], total_slots)
    wrapped = jnp.where(offset > total_slots - slots, offset - total_slots, batch)
    start = slots + jnp.where(offset < batch, offset, wrapped)
    place = jnp.stack([group, member, group % 2, start]).astype(jnp.int32)

    x = activations.transpose(1, 2, 0, 3).reshape(ROWS, OUT)
    spatial_weight = conv_spatial.reshape(3, 3 * MID, MID)
    table = shuffle.reshape(batch // KEY, KEY)
    x, spatial_weight, expand_weight, delta, mean, back, message = reduce_call(
        place, x, conv_reduce, table, queries, spatial_weight, conv_expand
    )
    received = lax.all_to_all(message, "member", split_axis=0, concat_axis=0, tiled=True)
    moments, units = block_call(received, spatial_weight, expand_weight)
    returned = lax.all_to_all(moments, "member", split_axis=0, concat_axis=0, tiled=True)
    copies = home_call(returned, back, mean, delta, spatial_weight, expand_weight, x, key_head, 2 * members)
    copies, units = lax.optimization_barrier((copies, units))
    logits = logits_call(units, negative_memory)
    same_core = [[g * members + m for g in (core, core + 2) for m in range(members)] for core in (0, 1)]
    near = lax.all_to_all(
        copies, ("group", "member"), split_axis=0, concat_axis=0, tiled=True, axis_index_groups=same_core
    )
    near, logits = lax.optimization_barrier((near, logits))
    far = lax.ppermute(near, "group", [(0, 1), (1, 0), (2, 3), (3, 2)])
    similarity = similarity_call(place, near, queries)
    new_queue = queue_call(place, near, far, negative_memory)
    return logits, similarity.reshape(IMAGES), new_queue


def solution(mesh):
    placed = (
        P(("group", "member"), None, None, None),
        P(),
        P(),
        P(),
        P(),
        P(),
        P(),
        P(("group", "member"), None),
        P("member", None),
    )
    return jax.shard_map(
        per_device,
        mesh=mesh,
        in_specs=placed,
        out_specs=(P("group", "member"), P(("group", "member")), P("member", None)),
        check_vma=False,
    )
```

```python
import jax
import jax.numpy as jnp
from jax import lax
from jax.experimental import pallas as pl
from jax.experimental.pallas import tpu as pltpu
from jax.sharding import PartitionSpec as P

norm_eps = 1e-05
unit_eps = 1e-06
sharpness_divisor = 0.2

IMAGES = 32
SIDE = 7
POSITIONS = SIDE * SIDE
ROW = SIDE * IMAGES
ROWS = POSITIONS * IMAGES
MID = 512
OUT = 2048
KEY = 128
SLAB = 8
SLABS = POSITIONS // SLAB
SIZE = SLAB * IMAGES
LAST = SLABS * MID
QUERIES = LAST + KEY
MESSAGE = QUERIES + MID
MOMENTS = 6 * KEY
MIB = 1 << 20
f32 = jnp.float32
bf16 = jnp.bfloat16


def iota(shape, dim):
    return lax.broadcasted_iota(jnp.int32, shape, dim)


def dot(a, b):
    return jnp.dot(a, b, preferred_element_type=f32)


def dot_tn(a, b):
    return lax.dot_general(a, b, (((0,), (0,)), ((), ())), preferred_element_type=f32)


def dot_nt(a, b):
    return lax.dot_general(a, b, (((1,), (1,)), ((), ())), preferred_element_type=f32)


def spread_select(select):
    left = (iota((SIZE, IMAGES), 0) // SLAB == iota((SIZE, IMAGES), 1)).astype(bf16)
    right = (iota((IMAGES, SIZE), 0) == iota((IMAGES, SIZE), 1) % IMAGES).astype(bf16)
    spread = dot(dot(left, select).astype(bf16), right)
    same = iota((SIZE, SIZE), 0) % SLAB == iota((SIZE, SIZE), 1) // IMAGES
    return jnp.where(same, spread, 0.0).astype(bf16)


def quarters(value):
    return jnp.concatenate([value[:, k * KEY : (k + 1) * KEY] for k in range(4)], axis=0)


def whole(pieces):
    return jnp.concatenate([pieces[k] for k in range(4)], axis=1)


def split(value):
    high = value.astype(bf16).astype(f32)
    return high, value - high


def unit_of(queries):
    query_f = queries.astype(f32)
    return query_f * lax.rsqrt(jnp.sum(query_f * query_f, axis=1, keepdims=True) + unit_eps)


def start_all(pairs, sems):
    copies = [pltpu.make_async_copy(a, b, sems.at[k]) for k, (a, b) in enumerate(pairs)]
    for copy in copies:
        copy.start()
    return copies


def peer_selector(place_ref, table):
    per_row = KEY // IMAGES
    block_rows = table[pl.ds(pl.multiple_of(place_ref[0] * SLAB, SLAB), SLAB), :]
    local = block_rows - (place_ref[0] * (IMAGES * IMAGES) + place_ref[1] * IMAGES)
    mine = jnp.logical_and(local >= 0, local < IMAGES)
    found = jnp.where(mine, local, 0).astype(f32).astype(bf16)
    by_block = (iota((IMAGES, SLAB), 0) // per_row == iota((IMAGES, SLAB), 1)).astype(bf16)
    inside = iota((IMAGES, KEY), 1) // IMAGES == iota((IMAGES, KEY), 0) % per_row
    chosen = jnp.sum(jnp.where(inside, dot(by_block, found), 0.0), axis=1, keepdims=True)
    return (chosen == iota((IMAGES, IMAGES), 1).astype(f32)).astype(bf16)


WAITS = {0: (0,), 1: (1, 2), 3: (3, 4, 5, 6)}


def reduce_kernel(
    place_ref, x_hbm, weight_hbm, table_hbm, query_hbm, spatial_hbm, expand_hbm,
    x, spatial_weight, expand_weight, delta, mean_ref, back_ref, message,
    weight, table, query, sems,
):
    map_rows = [pl.ds(y * ROW, ROW) for y in range(SIDE)]
    weight_rows = [pl.ds(k * MID, MID) for k in range(OUT // MID)]
    loads = start_all(
        [(table_hbm, table), (query_hbm, query)]
        + [(weight_hbm.at[rows, :], weight.at[rows, :]) for rows in weight_rows]
        + [(x_hbm.at[rows, :], x.at[rows, :]) for rows in map_rows]
        + [(spatial_hbm.at[k], spatial_weight.at[k]) for k in range(3)]
        + [(expand_hbm, expand_weight)],
        sems,
    )

    loads[0].wait()
    loads[1].wait()
    mover = spread_select(peer_selector(place_ref, table))
    same = (iota((SIZE, SIZE), 0) == iota((SIZE, SIZE), 1)).astype(bf16)
    back_ref[...] = dot_tn(mover, same).astype(bf16)
    unit = unit_of(query[...])
    unit = jnp.concatenate([unit[SLAB * k : SLAB * (k + 1)] for k in range(4)], axis=1)
    message[:, :, pl.ds(QUERIES, MID)] = jnp.broadcast_to(unit[None], (IMAGES, SLAB, MID)).astype(bf16)
    for copy in loads[2:6]:
        copy.wait()
    done = [0]
    parts = []

    def finish(y):
        delta[map_rows[y], :] = (parts[y] - mean_f[None]).reshape(ROW, MID).astype(bf16)
        while (done[0] + 1) * SLAB <= (y + 1) * SIDE:
            moved = dot(mover, delta[pl.ds(done[0] * SIZE, SIZE), :]).reshape(IMAGES, SLAB, MID)
            message[:, :, pl.ds(done[0] * MID, MID)] = moved.astype(bf16)
            done[0] += 1

    for y in range(SIDE):
        for k in WAITS.get(y, ()):
            loads[6 + k].wait()
        part = dot(x[map_rows[y], :], weight[...]).reshape(SIDE, IMAGES, MID)
        if y == 0:
            mean = (jnp.sum(part, axis=0) * (1.0 / SIDE)).astype(bf16)
            mean_f = mean.astype(f32)
            mean_ref[...] = mean
        if y > 0:
            finish(y - 1)
        parts.append(part)
    finish(SIDE - 1)
    last = jnp.concatenate([quarters(delta[pl.ds(SLABS * SIZE, IMAGES), :]), quarters(mean)], axis=0)
    message[:, :, pl.ds(LAST, KEY)] = dot(mover, last).reshape(IMAGES, SLAB, KEY).astype(bf16)
    for copy in loads[6 + SIDE :]:
        copy.wait()


def store_windows(windows, reduced, y):
    edge = jnp.zeros((IMAGES, MID), bf16)
    at = (y + 1) * ROW
    windows[pl.ds(at, IMAGES), pl.ds(0, MID)] = edge
    windows[pl.ds(at + IMAGES, ROW - IMAGES), pl.ds(0, MID)] = reduced[: ROW - IMAGES]
    windows[pl.ds(at, ROW), pl.ds(MID, MID)] = reduced
    windows[pl.ds(at, ROW - IMAGES), pl.ds(2 * MID, MID)] = reduced[IMAGES:]
    windows[pl.ds(at + ROW - IMAGES, IMAGES), pl.ds(2 * MID, MID)] = edge


def clear_border(windows):
    border = jnp.zeros((ROW, 3 * MID), bf16)
    windows[pl.ds(0, ROW), :] = border
    windows[pl.ds((SIDE + 1) * ROW, ROW), :] = border


def convolve_row(windows, spatial_weight, y):
    return dot(
        jnp.concatenate([windows[pl.ds((y + k) * ROW, ROW), :] for k in range(3)], axis=1),
        spatial_weight[...].reshape(9 * MID, MID),
    )


def fold(value):
    return jnp.sum(value.reshape(-1, IMAGES, value.shape[1]), axis=0)


def block_mean(total):
    return jnp.sum(total, axis=0, keepdims=True) * (1.0 / ROWS)


def block_kernel(received, spatial_weight, expand_weight, moments, units, values, windows, square_sums):
    clear_border(windows)
    row, column = iota((SIZE, SIZE), 0), iota((SIZE, SIZE), 1)
    mover = jnp.logical_and(row % IMAGES == column // SLAB, row // IMAGES == column % SLAB).astype(bf16)

    tail = dot(mover, received[:, :, pl.ds(LAST, KEY)].reshape(SIZE, KEY)).reshape(SLAB, IMAGES, KEY)
    mean = whole(tail[4:])
    shift = jnp.sum(mean, axis=0, keepdims=True) * (1.0 / IMAGES)
    away = mean - shift
    last = whole(tail[:4]) + away
    values[pl.ds(SLABS * SIZE, IMAGES), :] = last
    total, squares = last, last * last
    for slab in range(SLABS):
        moved = dot(mover, received[:, :, pl.ds(slab * MID, MID)].reshape(SIZE, MID))
        moved = (moved.reshape(SLAB, IMAGES, MID) + away[None]).reshape(SIZE, MID)
        values[pl.ds(slab * SIZE, SIZE), :] = moved
        total = total + fold(moved)
        squares = squares + fold(moved * moved)
    offset1 = block_mean(total)
    center1 = shift + offset1
    scale1 = lax.rsqrt(block_mean(squares) - offset1 * offset1 + norm_eps).astype(bf16).astype(f32)
    queries = received[:, :, pl.ds(QUERIES, MID)].astype(f32)
    queries = jnp.concatenate([queries[:, None, :, k * KEY : (k + 1) * KEY] for k in range(4)], axis=1)
    units[...] = queries.reshape(IMAGES * IMAGES, KEY).astype(bf16)

    def normalize(y):
        reduced = jnp.maximum((values[pl.ds(y * ROW, ROW), :] - offset1) * scale1, 0.0)
        store_windows(windows, reduced.astype(bf16), y)

    normalize(0)
    total = squares = jnp.zeros((IMAGES, MID), f32)
    for y in range(SIDE):
        if y + 1 < SIDE:
            normalize(y + 1)
        second = convolve_row(windows, spatial_weight, y)
        values[pl.ds(y * ROW, ROW), :] = second
        total = total + fold(second)
        squares = squares + fold(second * second)
    center2 = block_mean(total)
    scale2 = lax.rsqrt(block_mean(squares) - center2 * center2 + norm_eps).astype(bf16).astype(f32)
    total = jnp.zeros((IMAGES, MID), f32)
    parts = range(OUT // MID)
    for y in range(SIDE):
        kept = jnp.maximum((values[pl.ds(y * ROW, ROW), :] - center2) * scale2, 0.0).astype(bf16)
        total = total + fold(kept.astype(f32))
        for part in parts:
            third = dot(kept, expand_weight[:, pl.ds(part * MID, MID)])
            square = fold(third * third)
            square_sums[part] = square if y == 0 else square_sums[part] + square
    mean_high, mean_low = split(block_mean(total))
    scale3 = []
    for part in parts:
        weight = expand_weight[:, pl.ds(part * MID, MID)]
        center3 = dot(mean_high.astype(bf16), weight) + dot(mean_low.astype(bf16), weight)
        scale3.append(lax.rsqrt(block_mean(square_sums[part]) - center3 * center3 + norm_eps))

    vectors = [*split(center1), *split(center2), mean_high, mean_low, scale1, scale2, *scale3]
    vectors = [quarters(vector) for vector in vectors]
    tiles = [jnp.concatenate(vectors[k : k + 2], axis=0) for k in range(0, 12, 2)]
    packed = jnp.concatenate(tiles, axis=1)
    moments[...] = jnp.broadcast_to(packed[None], (IMAGES, SLAB, MOMENTS)).astype(bf16)


def home_kernel(
    received, back, mean, delta, spatial_weight, expand_weight, x, head,
    keys, windows, spatial, pooled,
):
    clear_border(windows)
    stats = dot(back[...], received[...].reshape(SIZE, MOMENTS))
    stats = stats.reshape(SLAB, IMAGES, MOMENTS)
    vectors = []
    for k in range(12):
        half, lanes = 4 * (k % 2), k // 2 * KEY
        vectors.append(whole([stats[half + q, :, lanes : lanes + KEY] for q in range(4)]))
    offset1 = mean[...].astype(f32) - (vectors[0] + vectors[1])
    center2 = vectors[2] + vectors[3]
    mean_high, mean_low = vectors[4].astype(bf16), vectors[5].astype(bf16)
    scale1, scale2 = vectors[6], vectors[7]

    def normalize(y):
        away = delta[pl.ds(y * ROW, ROW), :].astype(f32).reshape(SIDE, IMAGES, MID)
        reduced = jnp.maximum((away + offset1[None]) * scale1[None], 0.0)
        store_windows(windows, reduced.reshape(ROW, MID).astype(bf16), y)

    normalize(0)

    for y in range(SIDE):
        if y + 1 < SIDE:
            normalize(y + 1)
        second = convolve_row(windows, spatial_weight, y).reshape(SIDE, IMAGES, MID)
        kept = jnp.maximum((second - center2[None]) * scale2[None], 0.0)
        spatial[pl.ds(y * ROW, ROW), :] = kept.reshape(ROW, MID).astype(bf16)

    for part in range(OUT // MID):
        columns = pl.ds(part * MID, MID)
        weight = expand_weight[:, columns]
        center3 = dot(mean_high, weight) + dot(mean_low, weight)
        scale3 = vectors[8 + part]
        total = jnp.zeros((IMAGES, MID), f32)
        for y in range(SIDE):
            rows = pl.ds(y * ROW, ROW)
            third = dot(spatial[rows, :], weight).reshape(SIDE, IMAGES, MID)
            kept = x[rows, columns].astype(f32).reshape(SIDE, IMAGES, MID)
            merged = jnp.maximum((third - center3[None]) * scale3[None] + kept, 0.0)
            total = total + jnp.sum(merged, axis=0)
        pooled[:, columns] = (total * (1.0 / POSITIONS)).astype(bf16)
    projected = dot(pooled[...], head[...])
    key = projected * lax.rsqrt(jnp.sum(projected * projected, axis=1, keepdims=True) + unit_eps)
    key = key.astype(bf16)
    keys[...] = jnp.broadcast_to(key[None], keys.shape)


def logits_kernel(units_ref, memory_ref, out_ref):
    out_ref[...] = (dot_nt(units_ref[...], memory_ref[...]) * (1.0 / sharpness_divisor)).astype(bf16)


def queue_kernel(place_ref, near_ref, far_ref, memory, out_hbm, padded, out_ref, sems):
    slots = memory.shape[0]
    batch = 4 * IMAGES * IMAGES
    half = IMAGES * IMAGES
    core = place_ref[2]
    start = place_ref[3]
    empty = start == slots + batch

    @pl.when(empty)
    def _():
        keep = pltpu.make_async_copy(memory, out_hbm, sems.at[0])
        keep.start()
        keep.wait()

    @pl.when(jnp.logical_not(empty))
    def _():
        for high in range(2):
            for ref, which in ((near_ref, core), (far_ref, 1 - core)):
                at = pl.multiple_of(slots + (2 * high + which) * half, half)
                padded[pl.ds(at, half), :] = ref[pl.ds(high * half, half), :]
        edge = jnp.zeros((slots, KEY), bf16)
        padded[pl.ds(0, slots), :] = edge
        padded[pl.ds(slots + batch, slots), :] = edge
        padded[pl.ds(2 * slots + batch, ALIGN), :] = edge[:ALIGN]
        base = start // ALIGN * ALIGN
        inner = start - base
        pick = (iota((TILE, TILE + ALIGN), 1) == iota((TILE, TILE + ALIGN), 0) + inner).astype(bf16)
        stores = []
        for part in range(slots // TILE):
            rows = padded[pl.ds(pl.multiple_of(base + part * TILE, ALIGN), TILE + ALIGN), :]
            fresh = dot(pick, rows)
            index = start - slots + part * TILE + iota((TILE, KEY), 0)
            inside = jnp.logical_and(index >= 0, index < batch)
            old = memory[pl.ds(part * TILE, TILE), :].astype(f32)
            out_ref[pl.ds(part * TILE, TILE), :] = jnp.where(inside, fresh, old).astype(bf16)
            if (part + 1) * TILE % STORE == 0:
                rows = pl.ds((part + 1) * TILE - STORE, STORE)
                store = pltpu.make_async_copy(out_ref.at[rows, :], out_hbm.at[rows, :], sems.at[len(stores)])
                store.start()
                stores.append(store)
        for store in stores:
            store.wait()


STORE = 512
ALIGN = 16
TILE = 64


def params(mib):
    return pltpu.CompilerParams(vmem_limit_bytes=mib * MIB)


VMEM = pl.BlockSpec(memory_space=pltpu.VMEM)
SMEM = pl.BlockSpec(memory_space=pltpu.SMEM)
ANY = pl.BlockSpec(memory_space=pl.ANY)
HBM = pl.BlockSpec(memory_space=pltpu.HBM)


def shape(*dims, dtype=bf16):
    return jax.ShapeDtypeStruct(dims, dtype)


def scratch(*dims, dtype=bf16):
    return pltpu.VMEM(dims, dtype)


def dma(count):
    return pltpu.SemaphoreType.DMA((count,))


def in_hbm(*arrays):
    return [pltpu.with_memory_space_constraint(array, pltpu.HBM) for array in arrays]


def in_vmem(*arrays):
    return [pltpu.with_memory_space_constraint(array, pltpu.VMEM) for array in arrays]


def reduce_call(place, x, conv_reduce, table, queries, conv_spatial, conv_expand):
    return pl.pallas_call(
        reduce_kernel,
        in_specs=[SMEM] + [HBM] * 6,
        out_specs=[VMEM] * 7,
        out_shape=[
            scratch(ROWS, OUT),
            scratch(*conv_spatial.shape),
            scratch(MID, OUT),
            scratch(ROWS, MID),
            scratch(IMAGES, MID),
            scratch(SIZE, SIZE),
            scratch(IMAGES, SLAB, MESSAGE),
        ],
        scratch_shapes=[
            scratch(OUT, MID),
            scratch(*table.shape, dtype=jnp.int32),
            scratch(IMAGES, KEY),
            dma(10 + SIDE),
        ],
        compiler_params=params(24),
        name="reduce",
    )(place, *in_hbm(x, conv_reduce, table, queries, conv_spatial, conv_expand))


def block_call(received, spatial_weight, expand_weight):
    return pl.pallas_call(
        block_kernel,
        in_specs=[VMEM] * 3,
        out_specs=[VMEM, VMEM],
        out_shape=[scratch(IMAGES, SLAB, MOMENTS), scratch(IMAGES * IMAGES, KEY)],
        scratch_shapes=[
            scratch(ROWS, MID, dtype=f32),
            scratch(ROWS + 2 * ROW, 3 * MID),
            scratch(OUT // MID, IMAGES, MID, dtype=f32),
        ],
        compiler_params=params(30),
        name="block",
    )(*in_vmem(received, spatial_weight, expand_weight))


def home_call(received, back, mean, delta, spatial_weight, expand_weight, x, key_head, copies):
    return pl.pallas_call(
        home_kernel,
        in_specs=[VMEM] * 8,
        out_specs=VMEM,
        out_shape=scratch(copies, IMAGES, KEY),
        scratch_shapes=[
            scratch(ROWS + 2 * ROW, 3 * MID),
            scratch(ROWS, MID),
            scratch(IMAGES, OUT),
        ],
        compiler_params=params(30),
        name="home",
    )(*in_vmem(received, back, mean, delta, spatial_weight, expand_weight, x), key_head)


def logits_call(units, memory):
    rows, columns = units.shape[0], memory.shape[0]
    step = 128
    return pl.pallas_call(
        logits_kernel,
        grid=(rows // step,),
        in_specs=[
            pl.BlockSpec((step, KEY), lambda at: (at, 0)),
            pl.BlockSpec((columns, KEY), lambda at: (0, 0)),
        ],
        out_specs=pl.BlockSpec((step, columns), lambda at: (at, 0)),
        out_shape=shape(rows, columns),
        compiler_params=params(12),
        cost_estimate=pl.CostEstimate(
            flops=2 * rows * columns * KEY, bytes_accessed=2 * rows * columns, transcendentals=0
        ),
        name="logits",
    )(units, memory)


def similarity_kernel(place_ref, keys, query, similarity_ref):
    own_rows = (place_ref[0] // 2 * IMAGES + place_ref[1]) * IMAGES
    key = keys[pl.ds(pl.multiple_of(own_rows, IMAGES), IMAGES), :]
    pairs = dot_nt(unit_of(query[...]).astype(bf16), key)
    own = iota((IMAGES, IMAGES), 0) == iota((IMAGES, IMAGES), 1)
    similarity = jnp.sum(jnp.where(own, pairs, 0.0), axis=0, keepdims=True)
    similarity_ref[...] = similarity / sharpness_divisor


def similarity_call(place, near, queries):
    return pl.pallas_call(
        similarity_kernel,
        in_specs=[SMEM, VMEM, VMEM],
        out_specs=VMEM,
        out_shape=shape(1, IMAGES, dtype=f32),
        compiler_params=params(12),
        cost_estimate=pl.CostEstimate(flops=MIB, bytes_accessed=MIB, transcendentals=0),
        name="similarity",
    )(place, *in_vmem(near.reshape(-1, KEY)), queries)


def queue_call(place, near, far, memory):
    return pl.pallas_call(
        queue_kernel,
        in_specs=[SMEM, VMEM, VMEM, VMEM],
        out_specs=ANY,
        out_shape=shape(*memory.shape),
        scratch_shapes=[
            scratch(2 * memory.shape[0] + 4 * IMAGES * IMAGES + ALIGN, KEY),
            scratch(*memory.shape),
            dma(memory.shape[0] // STORE),
        ],
        compiler_params=params(32),
        name="queue",
    )(place, *in_vmem(near.reshape(-1, KEY), far.reshape(-1, KEY)), memory)


def per_device(
    activations, shuffle, pointer, conv_reduce, conv_spatial, conv_expand, key_head, queries, negative_memory
):
    group, member = lax.axis_index("group"), lax.axis_index("member")
    members = lax.axis_size("member")
    slots = negative_memory.shape[0]
    total_slots = slots * members
    batch = shuffle.shape[0]
    offset = jnp.mod(member * slots - pointer[0], total_slots)
    wrapped = jnp.where(offset > total_slots - slots, offset - total_slots, batch)
    start = slots + jnp.where(offset < batch, offset, wrapped)
    place = jnp.stack([group, member, group % 2, start]).astype(jnp.int32)

    x = activations.transpose(1, 2, 0, 3).reshape(ROWS, OUT)
    spatial_weight = conv_spatial.reshape(3, 3 * MID, MID)
    table = shuffle.reshape(batch // KEY, KEY)
    x, spatial_weight, expand_weight, delta, mean, back, message = reduce_call(
        place, x, conv_reduce, table, queries, spatial_weight, conv_expand
    )
    received = lax.all_to_all(message, "member", split_axis=0, concat_axis=0, tiled=True)
    moments, units = block_call(received, spatial_weight, expand_weight)
    returned = lax.all_to_all(moments, "member", split_axis=0, concat_axis=0, tiled=True)
    copies = home_call(returned, back, mean, delta, spatial_weight, expand_weight, x, key_head, 2 * members)
    copies, units = lax.optimization_barrier((copies, units))
    logits = logits_call(units, negative_memory)
    same_core = [[g * members + m for g in (core, core + 2) for m in range(members)] for core in (0, 1)]
    near = lax.all_to_all(
        copies, ("group", "member"), split_axis=0, concat_axis=0, tiled=True, axis_index_groups=same_core
    )
    near, logits = lax.optimization_barrier((near, logits))
    far = lax.ppermute(near, "group", [(0, 1), (1, 0), (2, 3), (3, 2)])
    similarity = similarity_call(place, near, queries)
    new_queue = queue_call(place, near, far, negative_memory)
    return logits, similarity.reshape(IMAGES), new_queue


def solution(mesh):
    placed = (
        P(("group", "member"), None, None, None),
        P(),
        P(),
        P(),
        P(),
        P(),
        P(),
        P(("group", "member"), None),
        P("member", None),
    )
    return jax.shard_map(
        per_device,
        mesh=mesh,
        in_specs=placed,
        out_specs=(P("group", "member"), P(("group", "member")), P("member", None)),
        check_vma=False,
    )
```
